32 devices in a mesh: seq: 16 (over z, x, core), head: 2 (over y).
Axes of the slice: x: 2, y: 2, z: 4, core: 2. Of those that a mesh axis runs over, the one named last changes fastest.
Arguments:
- doppler_input: bfloat16 [32, 256, 768], P('seq', None, 'head'), may hold values from -14 to 14
- range_saved_input: bfloat16 [32, 256, 768], P('seq', None, 'head'), may hold values from -14 to 14
- layer_cot: bfloat16 [32, 256, 768], P('seq', None, 'head'), may hold values from -6 to 6
- qkv_doppler: bfloat16 [768, 2304], P(None, 'head'), may hold values from -1 to 1
- out_doppler: bfloat16 [768, 768], P('head'), may hold values from -0.21875 to 0.21875
- qkv_range: bfloat16 [768, 2304], P(None, 'head'), may hold values from -1 to 1
- out_range: bfloat16 [768, 768], P('head'), may hold values from -0.21875 to 0.21875
Outputs:
- input_grad: bfloat16 [32, 256, 768], P('seq', None, 'head')
- qkv_doppler_grad: float32 [768, 2304], P('seq', 'head')
- out_doppler_grad: float32 [768, 768], P('head', 'seq')
- qkv_range_grad: float32 [768, 2304], P('seq', 'head')
- out_range_grad: float32 [768, 768], P('head', 'seq')
The draws below stay inside these ranges and needn't reach their ends.
All inputs are finite; a program needn't handle non-finite values.
Results may differ from the reference program's by a relative error of at most 0.014.
The reference program's roundings to bfloat16 on the way count: a program that leaves them out, or rounds other values in their place, can miss the bound.
Values may be sent and summed in bfloat16 or wider, within the bound.
A program may use at most 128 MiB of HBM per device.

```python
import jax
import jax.numpy as jnp
from jax import lax

D = 768
HEADS = 12
HD = 64
DOP = 256
RANGE = 32
GROUPS = 1
N_SEQ = 16


def block_factor(key):
    pairing = jax.random.permutation(key, N_SEQ)
    range_block = jnp.arange(RANGE) // (RANGE // N_SEQ)
    feature_block = jnp.arange(D) // (D // N_SEQ)
    chosen = feature_block[None, :] == pairing[range_block][:, None]
    return jnp.where(chosen, 4.0, 1.0)[:, None, :]


def draw_doppler_input(key, part):
    key = jax.random.fold_in(key, 11)
    pair_key = jax.random.fold_in(key, 5)
    factor = block_factor(pair_key)
    base = jax.random.truncated_normal(key, -3.5, 3.5, (RANGE, DOP, D), jnp.float32)
    return (base * factor).astype(jnp.bfloat16)


def draw_range_saved_input(key, part):
    key = jax.random.fold_in(key, 12)
    pair_key = jax.random.fold_in(key, 5)
    factor = block_factor(pair_key)
    base = jax.random.truncated_normal(key, -3.5, 3.5, (RANGE, DOP, D), jnp.float32)
    return (base * factor).astype(jnp.bfloat16)


def draw_qkv_doppler(key, part):
    key = jax.random.fold_in(key, 21)
    return (jax.random.truncated_normal(key, -4.0, 4.0, (D, 3 * D), jnp.float32) * D ** (-0.5)).astype(jnp.bfloat16)


def draw_qkv_range(key, part):
    key = jax.random.fold_in(key, 22)
    return (jax.random.truncated_normal(key, -4.0, 4.0, (D, 3 * D), jnp.float32) * D ** (-0.5)).astype(jnp.bfloat16)


def strengthened(values, stream_key, source, target, parts, factor):
    def block_of(dim):
        return (jnp.arange(values.shape[dim]) // (values.shape[dim] // parts)).reshape((-1,) + (1,) * (values.ndim - 1 - dim))

    one_side = jax.random.permutation(stream_key, parts)[block_of(target)]
    second = (block_of(target) + parts // 2) % parts
    return jnp.where((block_of(source) == one_side) | (block_of(source) == second), factor * values, values)


def level_of(own_key, extent, cuts, least, high):
    gain, own = 1.0, jax.random.fold_in(own_key, 6)
    for dim, blocks in cuts:
        draws = jnp.exp(jax.random.uniform(jax.random.fold_in(own, dim), (blocks,), jnp.float32, least / len(cuts), high / len(cuts)))
        gain = gain * jnp.repeat(draws, extent[dim] // blocks).reshape([-1 if axis == dim else 1 for axis in range(len(extent))])
    return gain


def centred(own_key, extent, width, limit, cuts=(), dtype=jnp.bfloat16):
    array = jax.random.normal(own_key, extent, jnp.float32) * width
    if len(cuts) > 0:
        array = level_of(own_key, extent, cuts, -0.22, 0.18) * array
    return jnp.clip(array, min=-limit, max=limit).astype(dtype)


def noise_with(key, extent, scale, reach, cuts, heavy, kind=jnp.bfloat16):
    result = scale * jax.random.normal(key, extent, jnp.float32)
    if cuts:
        result = result * level_of(key, extent, cuts, -0.22, 0.18)
    return jnp.clip(strengthened(result, jax.random.fold_in(key, 3), *heavy), -reach, reach).astype(kind)


def setup_inputs(seed: int = 0) -> dict:
    arg_keys = jax.random.split(jax.random.key(seed), 8)
    return {
        "doppler_input": draw_doppler_input(jax.random.fold_in(arg_keys[7], 71), 0),
        "range_saved_input": draw_range_saved_input(jax.random.fold_in(arg_keys[7], 71), 0),
        "layer_cot": noise_with(arg_keys[2], (RANGE, DOP, D), 1.0, 6.0, ((0, 16), (2, 2)), (0, 2, 16, 2.0)),
        "qkv_doppler": draw_qkv_doppler(jax.random.fold_in(arg_keys[7], 71), 0),
        "out_doppler": centred(arg_keys[4], (D, D), D ** -0.5, 0.21875, ((0, 2),)),
        "qkv_range": draw_qkv_range(jax.random.fold_in(arg_keys[7], 71), 0),
        "out_range": centred(arg_keys[6], (D, D), D ** -0.5, 0.21875, ((0, 2),)),
    }


DOPPLER_SHAPES = ("asu,avu->asv", "ojs,ost->ojt", "aru,ary->auy")
RANGE_SHAPES = ("mpw,cpw->pmc", "fdv,vfo->dfo", "nhr,hnp->rnp")


def rounded(value):
    return lax.optimization_barrier(value.astype(jnp.bfloat16)).astype(jnp.float32)


def head_backward(query, keys, values, grad_attn, forms, scale):
    query = query.astype(jnp.float32)
    keys = keys.astype(jnp.float32)
    values = values.astype(jnp.float32)
    grad_attn = grad_attn.astype(jnp.float32)
    scores = jnp.einsum(forms[0], query, keys) * scale
    scores = scores - jnp.max(scores, axis=-1, keepdims=True)
    expo = jnp.exp(scores)
    probs = expo / jnp.sum(expo, axis=-1, keepdims=True)
    probs_low = rounded(probs)
    attended = jnp.einsum(forms[1], probs_low, values).astype(jnp.bfloat16)
    grad_values = jnp.einsum(forms[2], probs_low, grad_attn).astype(jnp.bfloat16)
    grad_probs = jnp.einsum(forms[0], grad_attn, values)
    grad_scores = rounded(probs * (grad_probs - jnp.sum(probs * grad_probs, axis=-1, keepdims=True)) * scale)
    grad_query = jnp.einsum(forms[1], grad_scores, keys).astype(jnp.bfloat16)
    grad_keys = jnp.einsum(forms[2], grad_scores, query).astype(jnp.bfloat16)
    return attended, grad_query, grad_keys, grad_values


def sublayer_backward(inputs, cotangent, weight_qkv, weight_out, forms):
    row_count, column_count = inputs.shape[0], inputs.shape[1]
    flat_in = inputs.reshape(-1, D)
    flat_cot = cotangent.reshape(-1, D)
    projection = jnp.dot(flat_in, weight_qkv, preferred_element_type=jnp.float32).astype(jnp.bfloat16)
    projection = jnp.moveaxis(projection.reshape(row_count, column_count, HEADS, 3, HD), 2, 0)
    grad_attn = jnp.dot(flat_cot, weight_out.T, preferred_element_type=jnp.float32).astype(jnp.bfloat16)
    grad_attn = jnp.moveaxis(grad_attn.reshape(row_count, column_count, HEADS, HD), 2, 0)
    scale = HD ** -0.5

    def one_head(pieces):
        block, grad_block = pieces
        attended, grad_query, grad_keys, grad_values = head_backward(
            block[:, :, 0], block[:, :, 1], block[:, :, 2], grad_block, forms, scale)
        return attended, jnp.stack([grad_query, grad_keys, grad_values], axis=2)

    attended, grad_proj = lax.map(one_head, (projection, grad_attn))
    attended = jnp.moveaxis(attended, 0, 2).reshape(-1, D)
    grad_proj = jnp.moveaxis(grad_proj, 0, 2).reshape(-1, 3 * D)
    output_gradient = jnp.dot(attended.T, flat_cot, preferred_element_type=jnp.float32)
    qkv_grad = jnp.dot(flat_in.T, grad_proj, preferred_element_type=jnp.float32)
    group_width = 3 * D // GROUPS
    summed = jnp.zeros((flat_in.shape[0], D), jnp.float32)
    for group_index in range(GROUPS):
        lower = group_index * group_width
        group_part = jnp.dot(grad_proj[:, lower:lower + group_width], weight_qkv[:, lower:lower + group_width].T,
                             preferred_element_type=jnp.float32)
        summed = summed + rounded(group_part)
    return summed.reshape(row_count, column_count, D), qkv_grad, output_gradient


def reference(doppler_input, range_saved_input, layer_cot, qkv_doppler, out_doppler, qkv_range, out_range):
    range_back, qkv_range_grad, out_range_grad = sublayer_backward(
        range_saved_input, layer_cot, qkv_range, out_range, RANGE_SHAPES)
    cotangent_mid = (layer_cot.astype(jnp.float32) + rounded(range_back)).astype(jnp.bfloat16)
    doppler_back, qkv_doppler_grad, out_doppler_grad = sublayer_backward(
        doppler_input, cotangent_mid, qkv_doppler, out_doppler, DOPPLER_SHAPES)
    input_grad = (cotangent_mid.astype(jnp.float32) + doppler_back).astype(jnp.bfloat16)
    return input_grad, qkv_doppler_grad, out_doppler_grad, qkv_range_grad, out_range_grad
```

```python
import jax
import jax.numpy as jnp
from jax import lax
from jax.sharding import PartitionSpec as P

HD = 64


DOPPLER_SHAPES = ("asu,avu->asv", "ojs,ost->ojt", "aru,ary->auy")
RANGE_SHAPES = ("mpw,cpw->pmc", "fdv,vfo->dfo", "nhr,hnp->rnp")
LEAD_CONTRACT = (((0,), (0,)), ((), ()))
TAIL_CONTRACT = (((1,), (1,)), ((), ()))


def swapped(block, axis, stride):
    count = lax.axis_size(axis)
    route = []
    for low in range(count):
        high = low | 1 << stride
        if high != low and high < count:
            route += [(low, high), (high, low)]
    return lax.ppermute(block, axis, route)


def head_backward(query, keys, values, grad_attn, forms, scale):
    scores = jnp.einsum(forms[0], query, keys, preferred_element_type=jnp.float32) * scale
    scores = scores - jnp.max(scores, axis=-1, keepdims=True)
    expo = jnp.exp(scores)
    probs = expo / jnp.sum(expo, axis=-1, keepdims=True)
    probs_low = probs.astype(jnp.bfloat16)
    attended = jnp.einsum(forms[1], probs_low, values, preferred_element_type=jnp.float32).astype(
        jnp.bfloat16
    )
    grad_values = jnp.einsum(
        forms[2], probs_low, grad_attn, preferred_element_type=jnp.float32
    ).astype(jnp.bfloat16)
    grad_probs = jnp.einsum(forms[0], grad_attn, values, preferred_element_type=jnp.float32)
    grad_scores = (
        probs * (grad_probs - jnp.sum(probs * grad_probs, axis=-1, keepdims=True)) * scale
    ).astype(jnp.bfloat16)
    grad_query = jnp.einsum(forms[1], grad_scores, keys, preferred_element_type=jnp.float32).astype(
        jnp.bfloat16
    )
    grad_keys = jnp.einsum(forms[2], grad_scores, query, preferred_element_type=jnp.float32).astype(
        jnp.bfloat16
    )
    return (attended, grad_query, grad_keys, grad_values)


def sublayer_local(inputs, cotangent, weight_qkv, weight_out, forms):
    width = inputs.shape[-1]
    leading = inputs.shape[:-1]
    flat_in = inputs.reshape(-1, width)
    flat_cot = cotangent.reshape(-1, width)
    heads_here = weight_out.shape[0] // HD
    projection = jnp.dot(flat_in, weight_qkv, preferred_element_type=jnp.float32).astype(
        jnp.bfloat16
    )
    projection = projection.reshape(leading + (heads_here, 3, HD))
    grad_attn = lax.dot_general(
        flat_cot, weight_out, TAIL_CONTRACT, preferred_element_type=jnp.float32
    )
    grad_attn = grad_attn.astype(jnp.bfloat16).reshape(leading + (heads_here, HD))
    scale = HD ** (-0.5)
    attended_list = []
    grad_list = []
    for head_index in range(heads_here):
        attended, grad_query, grad_keys, grad_values = head_backward(
            projection[..., head_index, 0, :],
            projection[..., head_index, 1, :],
            projection[..., head_index, 2, :],
            grad_attn[..., head_index, :],
            forms,
            scale,
        )
        attended_list.append(attended)
        grad_list.append(jnp.stack([grad_query, grad_keys, grad_values], axis=-2))
    attended = jnp.stack(attended_list, axis=-2).reshape(-1, heads_here * HD)
    grad_proj = jnp.stack(grad_list, axis=-3).reshape(-1, 3 * heads_here * HD)
    out_term = lax.dot_general(
        attended, flat_cot, LEAD_CONTRACT, preferred_element_type=jnp.float32
    )
    qkv_term = lax.dot_general(
        flat_in, grad_proj, LEAD_CONTRACT, preferred_element_type=jnp.float32
    )
    group_part = lax.dot_general(
        grad_proj, weight_qkv, TAIL_CONTRACT, preferred_element_type=jnp.float32
    )
    return (group_part.astype(jnp.bfloat16).reshape(inputs.shape), qkv_term, out_term)


def pair_weights(weight_qkv, weight_out, lower_half):
    other_qkv = swapped(weight_qkv, "head", 0)
    other_out = swapped(weight_out, "head", 0)
    full_qkv = jnp.where(
        lower_half,
        jnp.concatenate([weight_qkv, other_qkv], 1),
        jnp.concatenate([other_qkv, weight_qkv], 1),
    )
    full_out = jnp.where(
        lower_half,
        jnp.concatenate([weight_out, other_out], 0),
        jnp.concatenate([other_out, weight_out], 0),
    )
    return (full_qkv, full_out)


def reduction_terms(qkv_term, out_term, lower_half):
    half_width = qkv_term.shape[1] // 2
    half_rows = out_term.shape[0] // 2
    qkv_low, qkv_high = (qkv_term[:, :half_width], qkv_term[:, half_width:])
    out_low, out_high = (out_term[:half_rows], out_term[half_rows:])
    qkv_keep = jnp.where(lower_half, qkv_low, qkv_high)
    qkv_send = jnp.where(lower_half, qkv_high, qkv_low)
    out_keep = jnp.where(lower_half, out_low, out_high)
    out_send = jnp.where(lower_half, out_high, out_low)
    qkv_term = qkv_keep + swapped(qkv_send.astype(jnp.bfloat16), "head", 0).astype(qkv_send.dtype)
    out_term = out_keep + swapped(out_send.astype(jnp.bfloat16), "head", 0).astype(out_send.dtype)
    return (
        lax.psum_scatter(qkv_term, "seq", scatter_dimension=0, tiled=True),
        lax.psum_scatter(out_term, "seq", scatter_dimension=1, tiled=True),
    )


def shards(
    doppler_input, range_saved_input, layer_cot, qkv_doppler, out_doppler, qkv_range, out_range
):
    head_count = lax.axis_size("head")
    group_count = head_count // 2
    split_count = head_count // group_count
    position = lax.axis_index("head") % split_count
    lower_half = position == 0
    range_qkv, range_out = pair_weights(qkv_range, out_range, lower_half)
    doppler_qkv, doppler_out = pair_weights(qkv_doppler, out_doppler, lower_half)
    full_mid, full_cot = (
        lax.all_gather(range_saved_input, "head", axis=2, tiled=True),
        lax.all_gather(layer_cot, "head", axis=2, tiled=True),
    )
    column_middle, column_cot = (
        lax.all_to_all(full_mid, "seq", split_axis=1, concat_axis=0, tiled=True),
        lax.all_to_all(full_cot, "seq", split_axis=1, concat_axis=0, tiled=True),
    )
    part_width = column_middle.shape[1] // split_count
    column_start = position * part_width
    local_mid = lax.dynamic_slice_in_dim(column_middle, column_start, part_width, 1)
    local_cot = lax.dynamic_slice_in_dim(column_cot, column_start, part_width, 1)
    range_part, qkv_term, out_term = sublayer_local(
        local_mid, local_cot, range_qkv, range_out, RANGE_SHAPES
    )
    qkv_range_grad, out_range_grad = reduction_terms(qkv_term, out_term, lower_half)
    column_moved = lax.all_to_all(range_part, "head", split_axis=2, concat_axis=1, tiled=True)
    column_moved = column_moved.reshape(
        column_moved.shape[0], group_count, -1, column_moved.shape[2]
    )
    range_back = jnp.sum(column_moved, axis=1, dtype=jnp.float32).astype(jnp.bfloat16)
    row_backward_result = lax.all_to_all(range_back, "seq", split_axis=0, concat_axis=1, tiled=True)
    cotangent_mid = (
        layer_cot.astype(jnp.float32) + row_backward_result.astype(jnp.float32)
    ).astype(jnp.bfloat16)
    full_in, full_cot_mid = (
        lax.all_gather(doppler_input, "head", axis=2, tiled=True),
        lax.all_gather(cotangent_mid, "head", axis=2, tiled=True),
    )
    part_rows = full_in.shape[0] // split_count
    row_start = position * part_rows
    local_in = lax.dynamic_slice_in_dim(full_in, row_start, part_rows, 0)
    local_cot_mid = lax.dynamic_slice_in_dim(full_cot_mid, row_start, part_rows, 0)
    doppler_part, qkv_term, out_term = sublayer_local(
        local_in, local_cot_mid, doppler_qkv, doppler_out, DOPPLER_SHAPES
    )
    qkv_doppler_grad, out_doppler_grad = reduction_terms(qkv_term, out_term, lower_half)
    row_moved = lax.all_to_all(doppler_part, "head", split_axis=2, concat_axis=0, tiled=True)
    row_moved = row_moved.reshape(group_count, -1, row_moved.shape[1], row_moved.shape[2])
    doppler_back = jnp.sum(row_moved, axis=0, dtype=jnp.float32)
    input_grad = (cotangent_mid.astype(jnp.float32) + doppler_back).astype(jnp.bfloat16)
    return (input_grad, qkv_doppler_grad, out_doppler_grad, qkv_range_grad, out_range_grad)


def both_halves(mine, other, lower_half):
    return jnp.where(
        lower_half, jnp.concatenate([mine, other], -1), jnp.concatenate([other, mine], -1)
    )


def heads_sublayer(inputs, cotangent, weight_qkv, weight_out, forms, lower_half):
    width = inputs.shape[-1]
    leading = inputs.shape[:-1]
    flat_in = inputs.reshape(-1, width)
    flat_cot = cotangent.reshape(-1, width)
    heads_here = weight_out.shape[0] // HD
    projection = jnp.dot(flat_in, weight_qkv, preferred_element_type=jnp.float32).astype(
        jnp.bfloat16
    )
    projection = projection.reshape(leading + (heads_here, 3, HD))
    grad_attn = lax.dot_general(
        flat_cot, weight_out, TAIL_CONTRACT, preferred_element_type=jnp.float32
    )
    grad_attn = grad_attn.astype(jnp.bfloat16).reshape(leading + (heads_here, HD))
    scale = HD ** (-0.5)
    attended_list = []
    grad_list = []
    for head_index in range(heads_here):
        attended, grad_query, grad_keys, grad_values = head_backward(
            projection[..., head_index, 0, :],
            projection[..., head_index, 1, :],
            projection[..., head_index, 2, :],
            grad_attn[..., head_index, :],
            forms,
            scale,
        )
        attended_list.append(attended)
        grad_list += [grad_query, grad_keys, grad_values]
    attended = jnp.concatenate(attended_list, axis=-1).reshape(-1, heads_here * HD)
    grad_proj = jnp.concatenate(grad_list, axis=-1).reshape(-1, 3 * heads_here * HD)
    out_term = lax.dot_general(
        flat_cot, attended, LEAD_CONTRACT, preferred_element_type=jnp.float32
    )
    qkv_term = lax.dot_general(
        flat_in, grad_proj, LEAD_CONTRACT, preferred_element_type=jnp.float32
    )
    part = lax.dot_general(
        grad_proj, weight_qkv, TAIL_CONTRACT, preferred_element_type=jnp.float32
    )
    half = width // 2
    keep = jnp.where(lower_half, part[:, :half], part[:, half:])
    send = jnp.where(lower_half, part[:, half:], part[:, :half])
    part = keep + swapped(send.astype(jnp.bfloat16), "head", 0).astype(jnp.float32)
    return (part.reshape(leading + (half,)), qkv_term, out_term)


def scattered_sum(term):
    count = lax.axis_size("seq")
    pieces = term.astype(jnp.bfloat16).reshape((count, -1) + term.shape[1:])
    pieces = lax.all_to_all(pieces, "seq", split_axis=0, concat_axis=0, tiled=True)
    return jnp.sum(pieces.astype(jnp.float32), axis=0)


def shards_by_head(
    doppler_input, range_saved_input, layer_cot, qkv_doppler, out_doppler, qkv_range, out_range
):
    lower_half = lax.axis_index("head") == 0
    both = jnp.stack([range_saved_input, layer_cot])
    both = lax.all_to_all(both, "seq", split_axis=2, concat_axis=1, tiled=True)
    both = both_halves(both, swapped(both, "head", 0), lower_half)
    part, qkv_term, out_term = heads_sublayer(
        both[0], both[1], qkv_range, out_range, RANGE_SHAPES, lower_half
    )
    range_back = part.astype(jnp.bfloat16)
    range_back = lax.all_to_all(range_back, "seq", split_axis=0, concat_axis=1, tiled=True)
    cotangent_mid = (layer_cot.astype(jnp.float32) + range_back.astype(jnp.float32)).astype(
        jnp.bfloat16
    )
    qkv_range_grad = scattered_sum(qkv_term)
    out_range_grad = scattered_sum(out_term).T
    full_in = both_halves(doppler_input, swapped(doppler_input, "head", 0), lower_half)
    full_cot = both_halves(cotangent_mid, swapped(cotangent_mid, "head", 0), lower_half)
    part, qkv_term, out_term = heads_sublayer(
        full_in, full_cot, qkv_doppler, out_doppler, DOPPLER_SHAPES, lower_half
    )
    input_grad = (
        cotangent_mid.astype(jnp.float32) + part.astype(jnp.bfloat16).astype(jnp.float32)
    ).astype(jnp.bfloat16)
    qkv_doppler_grad = scattered_sum(qkv_term)
    out_doppler_grad = scattered_sum(out_term).T
    return (input_grad, qkv_doppler_grad, out_doppler_grad, qkv_range_grad, out_range_grad)


def solution(mesh):
    placed = (
        P("seq", None, "head"),
        P("seq", None, "head"),
        P("seq", None, "head"),
        P(None, "head"),
        P("head", None),
        P(None, "head"),
        P("head", None),
    )
    return jax.shard_map(
        shards_by_head if mesh.shape["head"] == 2 else shards,
        mesh=mesh,
        in_specs=placed,
        out_specs=(
            P("seq", None, "head"),
            P("seq", "head"),
            P("head", "seq"),
            P("seq", "head"),
            P("head", "seq"),
        ),
        check_vma=False,
    )
```

```python
import functools

import jax
import jax.numpy as jnp
from jax import lax
from jax.experimental import pallas as pl
from jax.experimental.pallas import tpu as pltpu
from jax.sharding import PartitionSpec as P

HD = 64


DOPPLER_SHAPES = ("asu,avu->asv", "ojs,ost->ojt", "aru,ary->auy")
RANGE_SHAPES = ("mpw,cpw->pmc", "fdv,vfo->dfo", "nhr,hnp->rnp")
LEAD_CONTRACT = (((0,), (0,)), ((), ()))
TAIL_CONTRACT = (((1,), (1,)), ((), ()))


def swapped(block, axis, stride):
    count = lax.axis_size(axis)
    route = []
    for low in range(count):
        high = low | 1 << stride
        if high != low and high < count:
            route += [(low, high), (high, low)]
    return lax.ppermute(block, axis, route)


def head_backward(query, keys, values, grad_attn, forms, scale):
    scores = jnp.einsum(forms[0], query, keys, preferred_element_type=jnp.float32) * scale
    scores = scores - jnp.max(scores, axis=-1, keepdims=True)
    expo = jnp.exp(scores)
    probs = expo / jnp.sum(expo, axis=-1, keepdims=True)
    probs_low = probs.astype(jnp.bfloat16)
    attended = jnp.einsum(forms[1], probs_low, values, preferred_element_type=jnp.float32).astype(
        jnp.bfloat16
    )
    grad_values = jnp.einsum(
        forms[2], probs_low, grad_attn, preferred_element_type=jnp.float32
    ).astype(jnp.bfloat16)
    grad_probs = jnp.einsum(forms[0], grad_attn, values, preferred_element_type=jnp.float32)
    grad_scores = (
        probs * (grad_probs - jnp.sum(probs * grad_probs, axis=-1, keepdims=True)) * scale
    ).astype(jnp.bfloat16)
    grad_query = jnp.einsum(forms[1], grad_scores, keys, preferred_element_type=jnp.float32).astype(
        jnp.bfloat16
    )
    grad_keys = jnp.einsum(forms[2], grad_scores, query, preferred_element_type=jnp.float32).astype(
        jnp.bfloat16
    )
    return (attended, grad_query, grad_keys, grad_values)


def sublayer_local(inputs, cotangent, weight_qkv, weight_out, forms):
    width = inputs.shape[-1]
    leading = inputs.shape[:-1]
    flat_in = inputs.reshape(-1, width)
    flat_cot = cotangent.reshape(-1, width)
    heads_here = weight_out.shape[0] // HD
    projection = jnp.dot(flat_in, weight_qkv, preferred_element_type=jnp.float32).astype(
        jnp.bfloat16
    )
    projection = projection.reshape(leading + (heads_here, 3, HD))
    grad_attn = lax.dot_general(
        flat_cot, weight_out, TAIL_CONTRACT, preferred_element_type=jnp.float32
    )
    grad_attn = grad_attn.astype(jnp.bfloat16).reshape(leading + (heads_here, HD))
    scale = HD ** (-0.5)
    attended_list = []
    grad_list = []
    for head_index in range(heads_here):
        attended, grad_query, grad_keys, grad_values = head_backward(
            projection[..., head_index, 0, :],
            projection[..., head_index, 1, :],
            projection[..., head_index, 2, :],
            grad_attn[..., head_index, :],
            forms,
            scale,
        )
        attended_list.append(attended)
        grad_list.append(jnp.stack([grad_query, grad_keys, grad_values], axis=-2))
    attended = jnp.stack(attended_list, axis=-2).reshape(-1, heads_here * HD)
    grad_proj = jnp.stack(grad_list, axis=-3).reshape(-1, 3 * heads_here * HD)
    out_term = lax.dot_general(
        attended, flat_cot, LEAD_CONTRACT, preferred_element_type=jnp.float32
    )
    qkv_term = lax.dot_general(
        flat_in, grad_proj, LEAD_CONTRACT, preferred_element_type=jnp.float32
    )
    group_part = lax.dot_general(
        grad_proj, weight_qkv, TAIL_CONTRACT, preferred_element_type=jnp.float32
    )
    return (group_part.astype(jnp.bfloat16).reshape(inputs.shape), qkv_term, out_term)


def pair_weights(weight_qkv, weight_out, lower_half):
    other_qkv = swapped(weight_qkv, "head", 0)
    other_out = swapped(weight_out, "head", 0)
    full_qkv = jnp.where(
        lower_half,
        jnp.concatenate([weight_qkv, other_qkv], 1),
        jnp.concatenate([other_qkv, weight_qkv], 1),
    )
    full_out = jnp.where(
        lower_half,
        jnp.concatenate([weight_out, other_out], 0),
        jnp.concatenate([other_out, weight_out], 0),
    )
    return (full_qkv, full_out)


def reduction_terms(qkv_term, out_term, lower_half):
    half_width = qkv_term.shape[1] // 2
    half_rows = out_term.shape[0] // 2
    qkv_low, qkv_high = (qkv_term[:, :half_width], qkv_term[:, half_width:])
    out_low, out_high = (out_term[:half_rows], out_term[half_rows:])
    qkv_keep = jnp.where(lower_half, qkv_low, qkv_high)
    qkv_send = jnp.where(lower_half, qkv_high, qkv_low)
    out_keep = jnp.where(lower_half, out_low, out_high)
    out_send = jnp.where(lower_half, out_high, out_low)
    qkv_term = qkv_keep + swapped(qkv_send.astype(jnp.bfloat16), "head", 0).astype(qkv_send.dtype)
    out_term = out_keep + swapped(out_send.astype(jnp.bfloat16), "head", 0).astype(out_send.dtype)
    return (
        lax.psum_scatter(qkv_term, "seq", scatter_dimension=0, tiled=True),
        lax.psum_scatter(out_term, "seq", scatter_dimension=1, tiled=True),
    )


def shards(
    doppler_input, range_saved_input, layer_cot, qkv_doppler, out_doppler, qkv_range, out_range
):
    head_count = lax.axis_size("head")
    group_count = head_count // 2
    split_count = head_count // group_count
    position = lax.axis_index("head") % split_count
    lower_half = position == 0
    range_qkv, range_out = pair_weights(qkv_range, out_range, lower_half)
    doppler_qkv, doppler_out = pair_weights(qkv_doppler, out_doppler, lower_half)
    full_mid, full_cot = (
        lax.all_gather(range_saved_input, "head", axis=2, tiled=True),
        lax.all_gather(layer_cot, "head", axis=2, tiled=True),
    )
    column_middle, column_cot = (
        lax.all_to_all(full_mid, "seq", split_axis=1, concat_axis=0, tiled=True),
        lax.all_to_all(full_cot, "seq", split_axis=1, concat_axis=0, tiled=True),
    )
    part_width = column_middle.shape[1] // split_count
    column_start = position * part_width
    local_mid = lax.dynamic_slice_in_dim(column_middle, column_start, part_width, 1)
    local_cot = lax.dynamic_slice_in_dim(column_cot, column_start, part_width, 1)
    range_part, qkv_term, out_term = sublayer_local(
        local_mid, local_cot, range_qkv, range_out, RANGE_SHAPES
    )
    qkv_range_grad, out_range_grad = reduction_terms(qkv_term, out_term, lower_half)
    column_moved = lax.all_to_all(range_part, "head", split_axis=2, concat_axis=1, tiled=True)
    column_moved = column_moved.reshape(
        column_moved.shape[0], group_count, -1, column_moved.shape[2]
    )
    range_back = jnp.sum(column_moved, axis=1, dtype=jnp.float32).astype(jnp.bfloat16)
    row_backward_result = lax.all_to_all(range_back, "seq", split_axis=0, concat_axis=1, tiled=True)
    cotangent_mid = (
        layer_cot.astype(jnp.float32) + row_backward_result.astype(jnp.float32)
    ).astype(jnp.bfloat16)
    full_in, full_cot_mid = (
        lax.all_gather(doppler_input, "head", axis=2, tiled=True),
        lax.all_gather(cotangent_mid, "head", axis=2, tiled=True),
    )
    part_rows = full_in.shape[0] // split_count
    row_start = position * part_rows
    local_in = lax.dynamic_slice_in_dim(full_in, row_start, part_rows, 0)
    local_cot_mid = lax.dynamic_slice_in_dim(full_cot_mid, row_start, part_rows, 0)
    doppler_part, qkv_term, out_term = sublayer_local(
        local_in, local_cot_mid, doppler_qkv, doppler_out, DOPPLER_SHAPES
    )
    qkv_doppler_grad, out_doppler_grad = reduction_terms(qkv_term, out_term, lower_half)
    row_moved = lax.all_to_all(doppler_part, "head", split_axis=2, concat_axis=0, tiled=True)
    row_moved = row_moved.reshape(group_count, -1, row_moved.shape[1], row_moved.shape[2])
    doppler_back = jnp.sum(row_moved, axis=0, dtype=jnp.float32)
    input_grad = (cotangent_mid.astype(jnp.float32) + doppler_back).astype(jnp.bfloat16)
    return (input_grad, qkv_doppler_grad, out_doppler_grad, qkv_range_grad, out_range_grad)


MESH = pl.DeviceIdType.MESH
F32 = jnp.float32
BF16 = jnp.bfloat16
PLAIN = (((1,), (0,)), ((), ()))
HIDDEN = -1e30


def mm(a, b, form=PLAIN):
    return lax.dot_general(a, b, form, preferred_element_type=F32)


def attention_unit(query, keys, values, grad_attn, seq_mask):
    scale = HD ** (-0.5)
    scores = mm(query, keys, TAIL_CONTRACT) * scale
    if seq_mask is not None:
        scores = jnp.where(seq_mask, scores, HIDDEN)
    expo = jnp.exp(scores - jnp.max(scores, axis=-1, keepdims=True))
    probs = expo * (1.0 / jnp.sum(expo, axis=-1, keepdims=True))
    probs_low = probs.astype(BF16)
    attended = mm(probs_low, values)
    grad_values = mm(probs_low, grad_attn, LEAD_CONTRACT)
    grad_probs = mm(grad_attn, values, TAIL_CONTRACT)
    dots = jnp.sum(probs * grad_probs, axis=-1, keepdims=True)
    grad_scores = (probs * (grad_probs - dots) * scale).astype(BF16)
    grad_query = mm(grad_scores, keys)
    grad_keys = mm(grad_scores, query, LEAD_CONTRACT)
    return attended, (grad_query, grad_keys, grad_values)


def layer_kernel(
    seq,
    dop_ref,
    rng_ref,
    cot_ref,
    wqd_hbm,
    wod_hbm,
    wqr_hbm,
    wor_hbm,
    ig_ref,
    qd_ref,
    od_ref,
    qr_ref,
    or_ref,
    wq,
    wo,
    xr,
    xs,
    xt,
    pj32,
    ga32,
    pj,
    ga,
    gp,
    att,
    keep,
    psend,
    precv,
    order,
    rb,
    back,
    mid,
    gs,
    t1r,
    t1,
    t2r,
    t2,
    t3r,
    wsem,
    lsem,
    a2a_s,
    a2a_r,
    fwd_s,
    fwd_r,
    dx_sem,
    part_sem,
    back_s,
    back_r,
    mid_sem,
    rs12,
    rs3_s,
    rs3_r,
):
    s = lax.axis_index("seq")
    h = lax.axis_index("head")
    o = 1 - h
    rows, bins, half = rng_ref.shape
    span = bins // seq
    tokens = rows * bins
    block = tokens // 2
    pair = {"seq": s, "head": o}
    cols = wqr_hbm.shape[1]
    tiles = cols // half

    def at_seq(q):
        return {"seq": q, "head": h}

    def remote(src, dst, send, recv, where):
        return pltpu.make_async_remote_copy(
            src_ref=src,
            dst_ref=dst,
            send_sem=send,
            recv_sem=recv,
            device_id=(where["seq"], where["head"]),
            device_id_type=MESH,
        )

    loads = [
        pltpu.make_async_copy(wqr_hbm, wq.at[0], wsem.at[0]),
        pltpu.make_async_copy(wor_hbm, wo.at[0], wsem.at[1]),
        pltpu.make_async_copy(wqd_hbm, wq.at[1], wsem.at[2]),
        pltpu.make_async_copy(wod_hbm, wo.at[1], wsem.at[3]),
    ]
    for load in loads:
        load.start()

    barrier = pltpu.get_barrier_semaphore()

    @pl.loop(1, seq)
    def _(k):
        pl.semaphore_signal(
            barrier, inc=1, device_id=(lax.rem(s + k, seq), h), device_id_type=MESH
        )

    pl.semaphore_signal(barrier, inc=1, device_id=(s, o), device_id_type=MESH)
    pl.semaphore_wait(barrier, seq)

    sources = (rng_ref, cot_ref)

    def exchange(a, k):
        peer = lax.rem(s + k, seq)
        return remote(
            sources[a].at[:, pl.ds(pl.multiple_of(peer * span, span), span), :],
            xr.at[a, h, pl.ds(s * rows, rows)],
            a2a_s.at[a, k],
            a2a_r.at[a, k],
            at_seq(peer),
        )

    def forward(a, k):
        origin = lax.rem(s - k + seq, seq)
        place = xr.at[a, h, pl.ds(origin * rows, rows)]
        return remote(place, place, fwd_s.at[a, k], fwd_r.at[a, k], pair)

    @pl.loop(1, seq)
    def _(k):
        for a in range(2):
            exchange(a, k).start()

    for a in range(2):
        own = pltpu.make_async_copy(
            sources[a].at[:, pl.ds(pl.multiple_of(s * span, span), span), :],
            xr.at[a, h, pl.ds(s * rows, rows)],
            lsem.at[a],
        )
        own.start()
        own.wait()
        forward(a, 0).start()

    @pl.loop(1, seq)
    def _(k):
        for a in range(2):
            exchange(a, k).wait_recv()
            forward(a, k).start()

    dop_send = remote(dop_ref, xs.at[1, 0, h], dx_sem.at[0], dx_sem.at[1], pair)
    dop_send.start()
    dop_own = pltpu.make_async_copy(dop_ref, xs.at[1, 0, h], lsem.at[2])
    dop_own.start()

    def to_blocks(side):
        for a in range(2):
            moved = xr[a, side].astype(F32)
            for b in range(2):
                piece = moved[:, b * (span // 2) : (b + 1) * (span // 2), :]
                xs[0, a, side, b * block : (b + 1) * block, :] = piece.reshape(
                    block, half
                ).astype(BF16)

    def turn(sub, a, side):
        xt[sub, a, side] = xs[sub, a, side].T

    def project(sub, side, first):
        @pl.loop(0, tiles)
        def _(t):
            at = pl.ds(pl.multiple_of(t * half, half), half)
            term = mm(xs[sub, 0, side], wq[sub, pl.ds(pl.multiple_of(side * half, half), half), at])
            if first:
                pj32[:, at] = term
            else:
                pj[:, at] = (pj32[:, at] + term).astype(BF16)

    def project_cot(sub, side, first):
        at = pl.ds(pl.multiple_of(side * half, half), half)
        term = mm(xs[sub, 1, side], wo[sub, :, at], TAIL_CONTRACT)
        if first:
            ga32[...] = term
        else:
            ga[...] = (ga32[...] + term).astype(BF16)

    def attention(seq_mask):
        @pl.loop(0, tiles)
        def _(t):
            at = pl.ds(pl.multiple_of(t * half, half), half)
            at_out = pl.ds(pl.multiple_of(t * 2 * HD, 2 * HD), 2 * HD)
            for b in range(2):
                here = slice(b * block, (b + 1) * block)
                six = pj[here, at]
                two = ga[here, at_out]
                att_list, grad_list = [], []
                for i in range(2):
                    q, k, v = [six[:, (3 * i + j) * HD : (3 * i + j + 1) * HD] for j in range(3)]
                    attended, grads = attention_unit(
                        q, k, v, two[:, i * HD : (i + 1) * HD], seq_mask
                    )
                    att_list.append(attended)
                    grad_list += list(grads)
                att[here, at_out] = jnp.concatenate(att_list, -1).astype(BF16)
                gp[here, at] = jnp.concatenate(grad_list, -1).astype(BF16)

    def part_of(sub, side):
        return mm(gp[...], wq[sub, pl.ds(pl.multiple_of(side * half, half), half), :], TAIL_CONTRACT)

    def part_exchange(sub):
        return remote(
            psend.at[sub], precv.at[sub], part_sem.at[sub, 0], part_sem.at[sub, 1], pair
        )

    core = lax.rem(s, 2)
    xbit = lax.rem(s // 2, 2)
    z = s // 4
    zs = seq // 4
    chunk = 2 * half // seq
    width = cols + half

    def grads(sub):
        @pl.loop(0, tiles)
        def _(t):
            at = pl.ds(pl.multiple_of(t * half, half), half)
            for side in range(2):
                term = mm(xt[sub, 0, side], gp[:, at]).astype(BF16)
                gs[sub, side, :, :, :, at] = term.reshape(seq // 4, 2, chunk, half)

        for side in range(2):
            term = mm(xt[sub, 1, side], att[...]).astype(BF16)
            gs[sub, side, :, :, :, cols:] = term.reshape(seq // 4, 2, chunk, half)

    def rs_first(sub):
        return remote(
            gs.at[sub, :, :, 1 - core],
            t1r.at[sub],
            rs12.at[sub, 0],
            rs12.at[sub, 1],
            at_seq(s + 1 - 2 * core),
        )

    def rs_second(sub):
        return remote(
            t1.at[sub, :, 1 - xbit],
            t2r.at[sub],
            rs12.at[sub, 2],
            rs12.at[sub, 3],
            at_seq(s + 2 - 4 * xbit),
        )

    def rs_third(sub, k):
        to = lax.rem(z + k, zs)
        return remote(
            t2.at[sub, to],
            t3r.at[sub, k - 1],
            rs3_s.at[sub, k - 1],
            rs3_r.at[sub, k - 1],
            at_seq(to * 4 + lax.rem(s, 4)),
        )

    def rs_after_first(sub):
        rs_first(sub).wait_recv()
        for side in range(2):

            @pl.loop(0, seq // 4)
            def _(c):
                at = side * (seq // 4) + c
                total = gs[sub, side, c, core].astype(F32) + t1r[sub, side, c].astype(F32)
                t1[sub, at // 2, lax.rem(at, 2)] = total.astype(BF16)

        rs_second(sub).start()

    def rs_after_second(sub):
        rs_second(sub).wait_recv()

        @pl.loop(0, zs)
        def _(c):
            total = t1[sub, c, xbit].astype(F32) + t2r[sub, c].astype(F32)
            t2[sub, c] = total.astype(BF16)

        for k in range(1, zs):
            rs_third(sub, k).start()

    def rs_finish(sub, q_out, o_out):
        total = t2[sub, z].astype(F32)
        for k in range(1, zs):
            rs_third(sub, k).wait_recv()
            total = total + t3r[sub, k - 1].astype(F32)
        q_out[...] = total[:, :cols]
        o_out[...] = total[:, cols:]

    loads[0].wait()
    loads[1].wait()
    to_blocks(h)
    project(0, h, True)
    project_cot(0, h, True)
    turn(0, 0, h)
    turn(0, 1, h)

    @pl.loop(0, seq)
    def _(k):
        for a in range(2):
            forward(a, k).wait_recv()

    to_blocks(o)
    project(0, o, False)
    project_cot(0, o, False)
    row_ids = lax.broadcasted_iota(jnp.int32, (block, block), 0)
    col_ids = lax.broadcasted_iota(jnp.int32, (block, block), 1)
    lane = span // 2
    attention(lax.rem(row_ids, lane) == lax.rem(col_ids, lane))
    psend[0] = part_of(0, o).astype(BF16)
    part_exchange(0).start()
    keep[...] = part_of(0, h)
    turn(0, 0, o)
    turn(0, 1, o)
    part_exchange(0).wait_recv()
    for b in range(2):
        here = slice(b * block, (b + 1) * block)
        total = keep[here, :] + precv[0, here, :].astype(F32)
        order[:, b * lane : (b + 1) * lane, :] = total.reshape(block // lane, lane, half)
    rb[...] = order[...].astype(BF16)

    def give_back(k):
        peer = lax.rem(s + k, seq)
        return remote(
            rb.at[pl.ds(peer * rows, rows)],
            back.at[:, pl.ds(pl.multiple_of(s * span, span), span), :],
            back_s.at[k],
            back_r.at[k],
            at_seq(peer),
        )

    @pl.loop(1, seq)
    def _(k):
        give_back(k).start()

    back_own = pltpu.make_async_copy(
        rb.at[pl.ds(s * rows, rows)],
        back.at[:, pl.ds(pl.multiple_of(s * span, span), span), :],
        lsem.at[3],
    )
    back_own.start()
    grads(0)
    back_own.wait()

    @pl.loop(1, seq)
    def _(k):
        give_back(k).wait_recv()

    for r in range(rows):
        new = cot_ref[r].astype(F32) + back[r].astype(F32)
        mid[r * bins : (r + 1) * bins, :] = new.astype(BF16)
    mid_send = remote(mid, xs.at[1, 1, h], mid_sem.at[0], mid_sem.at[1], pair)
    mid_send.start()
    rs_first(0).start()
    xs[1, 1, h] = mid[...]
    loads[2].wait()
    loads[3].wait()
    dop_own.wait()
    project(1, h, True)
    project_cot(1, h, True)
    dop_send.wait_recv()
    project(1, o, False)
    rs_after_first(0)
    for side in range(2):
        turn(1, 0, side)
    turn(1, 1, h)
    mid_send.wait_recv()
    project_cot(1, o, False)
    rs_after_second(0)
    attention(None)
    turn(1, 1, o)
    grads(1)
    rs_first(1).start()
    psend[1] = part_of(1, o).astype(BF16)
    part_exchange(1).start()
    rs_after_first(1)
    keep[...] = part_of(1, h)
    rs_finish(0, qr_ref, or_ref)
    part_exchange(1).wait_recv()
    added = (keep[...] + precv[1].astype(F32)).astype(BF16).astype(F32)
    ig_ref[...] = (mid[...].astype(F32) + added).astype(BF16)
    rs_after_second(1)
    rs_finish(1, qd_ref, od_ref)

    @pl.loop(1, seq)
    def _(k):
        for a in range(2):
            exchange(a, k).wait_send()
        give_back(k).wait_send()

    @pl.loop(0, seq)
    def _(k):
        for a in range(2):
            forward(a, k).wait_send()

    dop_send.wait_send()
    mid_send.wait_send()
    for sub in range(2):
        part_exchange(sub).wait_send()
        rs_first(sub).wait_send()
        rs_second(sub).wait_send()
        for k in range(1, zs):
            rs_third(sub, k).wait_send()


def shards_by_head(
    doppler_input, range_saved_input, layer_cot, qkv_doppler, out_doppler, qkv_range, out_range
):
    seq = lax.axis_size("seq")
    rows, bins, half = layer_cot.shape
    tokens = rows * bins
    cols = qkv_range.shape[1]
    chunk = 2 * half // seq
    width = cols + half
    span = bins // seq
    dma = pltpu.SemaphoreType.DMA
    vmem = pl.BlockSpec(memory_space=pltpu.VMEM)
    hbm = pl.BlockSpec(memory_space=pl.ANY)
    zs = seq // 4
    scratch = [
        pltpu.VMEM((2, 2 * half, cols), BF16),
        pltpu.VMEM((2, half, 2 * half), BF16),
        pltpu.VMEM((2, 2, rows * seq, span, half), BF16),
        pltpu.VMEM((2, 2, 2, tokens, half), BF16),
        pltpu.VMEM((2, 2, 2, half, tokens), BF16),
        pltpu.VMEM((tokens, cols), F32),
        pltpu.VMEM((tokens, half), F32),
        pltpu.VMEM((tokens, cols), BF16),
        pltpu.VMEM((tokens, half), BF16),
        pltpu.VMEM((tokens, cols), BF16),
        pltpu.VMEM((tokens, half), BF16),
        pltpu.VMEM((tokens, half), F32),
        pltpu.VMEM((2, tokens, half), BF16),
        pltpu.VMEM((2, tokens, half), BF16),
        pltpu.VMEM((rows * seq, span, half), F32),
        pltpu.VMEM((rows * seq, span, half), BF16),
        pltpu.VMEM((rows, bins, half), BF16),
        pltpu.VMEM((tokens, half), BF16),
        pltpu.VMEM((2, 2, seq // 4, 2, chunk, width), BF16),
        pltpu.VMEM((2, 2, seq // 4, chunk, width), BF16),
        pltpu.VMEM((2, zs, 2, chunk, width), BF16),
        pltpu.VMEM((2, zs, chunk, width), BF16),
        pltpu.VMEM((2, zs, chunk, width), BF16),
        pltpu.VMEM((2, zs - 1, chunk, width), BF16),
        dma((4,)),
        dma((4,)),
        dma((2, seq)),
        dma((2, seq)),
        dma((2, seq)),
        dma((2, seq)),
        dma((2,)),
        dma((2, 2)),
        dma((seq,)),
        dma((seq,)),
        dma((2,)),
        dma((2, 4)),
        dma((2, zs - 1)),
        dma((2, zs - 1)),
    ]
    ig, qd, od, qr, out_r = pl.pallas_call(
        functools.partial(layer_kernel, seq),
        out_shape=(
            jax.ShapeDtypeStruct((tokens, half), BF16),
            jax.ShapeDtypeStruct((chunk, cols), F32),
            jax.ShapeDtypeStruct((chunk, half), F32),
            jax.ShapeDtypeStruct((chunk, cols), F32),
            jax.ShapeDtypeStruct((chunk, half), F32),
        ),
        in_specs=[vmem] * 3 + [hbm] * 4,
        out_specs=(vmem,) * 5,
        scratch_shapes=scratch,
        compiler_params=pltpu.CompilerParams(
            collective_id=0, has_side_effects=True, vmem_limit_bytes=56 * 2**20
        ),
        name="axial_backward",
    )(
        doppler_input.reshape(tokens, half),
        range_saved_input,
        layer_cot,
        qkv_doppler,
        out_doppler,
        qkv_range,
        out_range,
    )
    return (ig.reshape(layer_cot.shape), qd, od.T, qr, out_r.T)


def by_head(mesh):
    return mesh.shape["head"] == 2 and mesh.shape["seq"] == 16


def solution(mesh):
    placed = (
        P("seq", None, "head"),
        P("seq", None, "head"),
        P("seq", None, "head"),
        P(None, "head"),
        P("head", None),
        P(None, "head"),
        P("head", None),
    )
    return jax.shard_map(
        shards_by_head if by_head(mesh) else shards,
        mesh=mesh,
        in_specs=placed,
        out_specs=(
            P("seq", None, "head"),
            P("seq", "head"),
            P("head", "seq"),
            P("seq", "head"),
            P("head", "seq"),
        ),
        check_vma=False,
    )
```

```python
import functools

import jax
import jax.numpy as jnp
from jax import lax
from jax.experimental import pallas as pl
from jax.experimental.pallas import tpu as pltpu
from jax.sharding import PartitionSpec as P

HD = 64


DOPPLER_SHAPES = ("asu,avu->asv", "ojs,ost->ojt", "aru,ary->auy")
RANGE_SHAPES = ("mpw,cpw->pmc", "fdv,vfo->dfo", "nhr,hnp->rnp")
LEAD_CONTRACT = (((0,), (0,)), ((), ()))
TAIL_CONTRACT = (((1,), (1,)), ((), ()))


def swapped(block, axis, stride):
    count = lax.axis_size(axis)
    route = []
    for low in range(count):
        high = low | 1 << stride
        if high != low and high < count:
            route += [(low, high), (high, low)]
    return lax.ppermute(block, axis, route)


def head_backward(query, keys, values, grad_attn, forms, scale):
    scores = jnp.einsum(forms[0], query, keys, preferred_element_type=jnp.float32) * scale
    scores = scores - jnp.max(scores, axis=-1, keepdims=True)
    expo = jnp.exp(scores)
    probs = expo / jnp.sum(expo, axis=-1, keepdims=True)
    probs_low = probs.astype(jnp.bfloat16)
    attended = jnp.einsum(forms[1], probs_low, values, preferred_element_type=jnp.float32).astype(
        jnp.bfloat16
    )
    grad_values = jnp.einsum(
        forms[2], probs_low, grad_attn, preferred_element_type=jnp.float32
    ).astype(jnp.bfloat16)
    grad_probs = jnp.einsum(forms[0], grad_attn, values, preferred_element_type=jnp.float32)
    grad_scores = (
        probs * (grad_probs - jnp.sum(probs * grad_probs, axis=-1, keepdims=True)) * scale
    ).astype(jnp.bfloat16)
    grad_query = jnp.einsum(forms[1], grad_scores, keys, preferred_element_type=jnp.float32).astype(
        jnp.bfloat16
    )
    grad_keys = jnp.einsum(forms[2], grad_scores, query, preferred_element_type=jnp.float32).astype(
        jnp.bfloat16
    )
    return (attended, grad_query, grad_keys, grad_values)


def sublayer_local(inputs, cotangent, weight_qkv, weight_out, forms):
    width = inputs.shape[-1]
    leading = inputs.shape[:-1]
    flat_in = inputs.reshape(-1, width)
    flat_cot = cotangent.reshape(-1, width)
    heads_here = weight_out.shape[0] // HD
    projection = jnp.dot(flat_in, weight_qkv, preferred_element_type=jnp.float32).astype(
        jnp.bfloat16
    )
    projection = projection.reshape(leading + (heads_here, 3, HD))
    grad_attn = lax.dot_general(
        flat_cot, weight_out, TAIL_CONTRACT, preferred_element_type=jnp.float32
    )
    grad_attn = grad_attn.astype(jnp.bfloat16).reshape(leading + (heads_here, HD))
    scale = HD ** (-0.5)
    attended_list = []
    grad_list = []
    for head_index in range(heads_here):
        attended, grad_query, grad_keys, grad_values = head_backward(
            projection[..., head_index, 0, :],
            projection[..., head_index, 1, :],
            projection[..., head_index, 2, :],
            grad_attn[..., head_index, :],
            forms,
            scale,
        )
        attended_list.append(attended)
        grad_list.append(jnp.stack([grad_query, grad_keys, grad_values], axis=-2))
    attended = jnp.stack(attended_list, axis=-2).reshape(-1, heads_here * HD)
    grad_proj = jnp.stack(grad_list, axis=-3).reshape(-1, 3 * heads_here * HD)
    out_term = lax.dot_general(
        attended, flat_cot, LEAD_CONTRACT, preferred_element_type=jnp.float32
    )
    qkv_term = lax.dot_general(
        flat_in, grad_proj, LEAD_CONTRACT, preferred_element_type=jnp.float32
    )
    group_part = lax.dot_general(
        grad_proj, weight_qkv, TAIL_CONTRACT, preferred_element_type=jnp.float32
    )
    return (group_part.astype(jnp.bfloat16).reshape(inputs.shape), qkv_term, out_term)


def pair_weights(weight_qkv, weight_out, lower_half):
    other_qkv = swapped(weight_qkv, "head", 0)
    other_out = swapped(weight_out, "head", 0)
    full_qkv = jnp.where(
        lower_half,
        jnp.concatenate([weight_qkv, other_qkv], 1),
        jnp.concatenate([other_qkv, weight_qkv], 1),
    )
    full_out = jnp.where(
        lower_half,
        jnp.concatenate([weight_out, other_out], 0),
        jnp.concatenate([other_out, weight_out], 0),
    )
    return (full_qkv, full_out)


def reduction_terms(qkv_term, out_term, lower_half):
    half_width = qkv_term.shape[1] // 2
    half_rows = out_term.shape[0] // 2
    qkv_low, qkv_high = (qkv_term[:, :half_width], qkv_term[:, half_width:])
    out_low, out_high = (out_term[:half_rows], out_term[half_rows:])
    qkv_keep = jnp.where(lower_half, qkv_low, qkv_high)
    qkv_send = jnp.where(lower_half, qkv_high, qkv_low)
    out_keep = jnp.where(lower_half, out_low, out_high)
    out_send = jnp.where(lower_half, out_high, out_low)
    qkv_term = qkv_keep + swapped(qkv_send.astype(jnp.bfloat16), "head", 0).astype(qkv_send.dtype)
    out_term = out_keep + swapped(out_send.astype(jnp.bfloat16), "head", 0).astype(out_send.dtype)
    return (
        lax.psum_scatter(qkv_term, "seq", scatter_dimension=0, tiled=True),
        lax.psum_scatter(out_term, "seq", scatter_dimension=1, tiled=True),
    )


def shards(
    doppler_input, range_saved_input, layer_cot, qkv_doppler, out_doppler, qkv_range, out_range
):
    head_count = lax.axis_size("head")
    group_count = head_count // 2
    split_count = head_count // group_count
    position = lax.axis_index("head") % split_count
    lower_half = position == 0
    range_qkv, range_out = pair_weights(qkv_range, out_range, lower_half)
    doppler_qkv, doppler_out = pair_weights(qkv_doppler, out_doppler, lower_half)
    full_mid, full_cot = (
        lax.all_gather(range_saved_input, "head", axis=2, tiled=True),
        lax.all_gather(layer_cot, "head", axis=2, tiled=True),
    )
    column_middle, column_cot = (
        lax.all_to_all(full_mid, "seq", split_axis=1, concat_axis=0, tiled=True),
        lax.all_to_all(full_cot, "seq", split_axis=1, concat_axis=0, tiled=True),
    )
    part_width = column_middle.shape[1] // split_count
    column_start = position * part_width
    local_mid = lax.dynamic_slice_in_dim(column_middle, column_start, part_width, 1)
    local_cot = lax.dynamic_slice_in_dim(column_cot, column_start, part_width, 1)
    range_part, qkv_term, out_term = sublayer_local(
        local_mid, local_cot, range_qkv, range_out, RANGE_SHAPES
    )
    qkv_range_grad, out_range_grad = reduction_terms(qkv_term, out_term, lower_half)
    column_moved = lax.all_to_all(range_part, "head", split_axis=2, concat_axis=1, tiled=True)
    column_moved = column_moved.reshape(
        column_moved.shape[0], group_count, -1, column_moved.shape[2]
    )
    range_back = jnp.sum(column_moved, axis=1, dtype=jnp.float32).astype(jnp.bfloat16)
    row_backward_result = lax.all_to_all(range_back, "seq", split_axis=0, concat_axis=1, tiled=True)
    cotangent_mid = (
        layer_cot.astype(jnp.float32) + row_backward_result.astype(jnp.float32)
    ).astype(jnp.bfloat16)
    full_in, full_cot_mid = (
        lax.all_gather(doppler_input, "head", axis=2, tiled=True),
        lax.all_gather(cotangent_mid, "head", axis=2, tiled=True),
    )
    part_rows = full_in.shape[0] // split_count
    row_start = position * part_rows
    local_in = lax.dynamic_slice_in_dim(full_in, row_start, part_rows, 0)
    local_cot_mid = lax.dynamic_slice_in_dim(full_cot_mid, row_start, part_rows, 0)
    doppler_part, qkv_term, out_term = sublayer_local(
        local_in, local_cot_mid, doppler_qkv, doppler_out, DOPPLER_SHAPES
    )
    qkv_doppler_grad, out_doppler_grad = reduction_terms(qkv_term, out_term, lower_half)
    row_moved = lax.all_to_all(doppler_part, "head", split_axis=2, concat_axis=0, tiled=True)
    row_moved = row_moved.reshape(group_count, -1, row_moved.shape[1], row_moved.shape[2])
    doppler_back = jnp.sum(row_moved, axis=0, dtype=jnp.float32)
    input_grad = (cotangent_mid.astype(jnp.float32) + doppler_back).astype(jnp.bfloat16)
    return (input_grad, qkv_doppler_grad, out_doppler_grad, qkv_range_grad, out_range_grad)


MESH = pl.DeviceIdType.MESH
F32 = jnp.float32
BF16 = jnp.bfloat16
PLAIN = (((1,), (0,)), ((), ()))
HIDDEN = -1e30


def mm(a, b, form=PLAIN):
    return lax.dot_general(a, b, form, preferred_element_type=F32)


def attention_unit(query, keys, values, grad_attn, seq_mask):
    scale = HD ** (-0.5)
    scores = mm(query, keys, TAIL_CONTRACT) * scale
    if seq_mask is not None:
        scores = jnp.where(seq_mask, scores, HIDDEN)
    expo = jnp.exp(scores - jnp.max(scores, axis=-1, keepdims=True))
    probs = expo * (1.0 / jnp.sum(expo, axis=-1, keepdims=True))
    probs_low = probs.astype(BF16)
    attended = mm(probs_low, values)
    grad_values = mm(probs_low, grad_attn, LEAD_CONTRACT)
    grad_probs = mm(grad_attn, values, TAIL_CONTRACT)
    dots = jnp.sum(probs * grad_probs, axis=-1, keepdims=True)
    grad_scores = (probs * (grad_probs - dots) * scale).astype(BF16)
    grad_query = mm(grad_scores, keys)
    grad_keys = mm(grad_scores, query, LEAD_CONTRACT)
    return attended, (grad_query, grad_keys, grad_values)


def layer_kernel(
    seq,
    dop_ref,
    rng_ref,
    cot_ref,
    wqd_hbm,
    wod_hbm,
    wqr_hbm,
    wor_hbm,
    ig_ref,
    qd_ref,
    od_ref,
    qr_ref,
    or_ref,
    wq,
    wo,
    xr,
    xs,
    xt,
    pj32,
    ga32,
    pj,
    ga,
    gp,
    att,
    keep,
    psend,
    precv,
    order,
    rb,
    back,
    mid,
    gs,
    t1r,
    t1,
    t2r,
    t2,
    t3r,
    wsem,
    lsem,
    a2a_s,
    a2a_r,
    fwd_s,
    fwd_r,
    dx_sem,
    part_sem,
    back_s,
    back_r,
    mid_sem,
    rs12,
    rs3_s,
    rs3_r,
):
    s = lax.axis_index("seq")
    h = lax.axis_index("head")
    o = 1 - h
    rows, bins, half = rng_ref.shape
    span = bins // seq
    tokens = rows * bins
    block = tokens // 2
    pair = {"seq": s, "head": o}
    cols = wqr_hbm.shape[1]
    tiles = cols // half
    lanes = 128
    cuts = half // lanes
    pieces = tiles + 1

    def at_seq(q):
        return {"seq": q, "head": h}

    def remote(src, dst, send, recv, where):
        return pltpu.make_async_remote_copy(
            src_ref=src,
            dst_ref=dst,
            send_sem=send,
            recv_sem=recv,
            device_id=(where["seq"], where["head"]),
            device_id_type=MESH,
        )

    loads = [
        pltpu.make_async_copy(wqr_hbm, wq.at[0], wsem.at[0]),
        pltpu.make_async_copy(wor_hbm, wo.at[0], wsem.at[1]),
        pltpu.make_async_copy(wqd_hbm, wq.at[1], wsem.at[2]),
        pltpu.make_async_copy(wod_hbm, wo.at[1], wsem.at[3]),
    ]
    for load in loads:
        load.start()

    barrier = pltpu.get_barrier_semaphore()

    @pl.loop(1, seq)
    def _(k):
        pl.semaphore_signal(
            barrier, inc=1, device_id=(lax.rem(s + k, seq), h), device_id_type=MESH
        )

    pl.semaphore_signal(barrier, inc=1, device_id=(s, o), device_id_type=MESH)
    pl.semaphore_wait(barrier, seq)

    sources = (rng_ref, cot_ref)

    def exchange(a, k):
        peer = lax.rem(s + k, seq)
        return remote(
            sources[a].at[:, pl.ds(pl.multiple_of(peer * span, span), span), :],
            xr.at[a, h, pl.ds(s * rows, rows)],
            a2a_s.at[a, k],
            a2a_r.at[a, k],
            at_seq(peer),
        )

    def forward(a, k):
        origin = lax.rem(s - k + seq, seq)
        place = xr.at[a, h, pl.ds(origin * rows, rows)]
        return remote(place, place, fwd_s.at[a, k], fwd_r.at[a, k], pair)

    @pl.loop(1, seq)
    def _(k):
        for a in range(2):
            exchange(a, k).start()

    for a in range(2):
        own = pltpu.make_async_copy(
            sources[a].at[:, pl.ds(pl.multiple_of(s * span, span), span), :],
            xr.at[a, h, pl.ds(s * rows, rows)],
            lsem.at[a],
        )
        own.start()
        own.wait()
        forward(a, 0).start()

    @pl.loop(1, seq)
    def _(k):
        for a in range(2):
            exchange(a, k).wait_recv()
            forward(a, k).start()

    dop_send = remote(dop_ref, xs.at[1, 0, h], dx_sem.at[0], dx_sem.at[1], pair)
    dop_send.start()
    dop_own = pltpu.make_async_copy(dop_ref, xs.at[1, 0, h], lsem.at[2])
    dop_own.start()

    def to_blocks(side):
        for a in range(2):
            moved = xr[a, side].astype(F32)
            for b in range(2):
                piece = moved[:, b * (span // 2) : (b + 1) * (span // 2), :]
                xs[0, a, side, b * block : (b + 1) * block, :] = piece.reshape(
                    block, half
                ).astype(BF16)

    def turn(sub, a, side):
        xt[sub, a, side] = xs[sub, a, side].T

    def project(sub, side, first):
        @pl.loop(0, tiles)
        def _(t):
            at = pl.ds(pl.multiple_of(t * half, half), half)
            term = mm(xs[sub, 0, side], wq[sub, pl.ds(pl.multiple_of(side * half, half), half), at])
            if first:
                pj32[:, at] = term
            else:
                pj[:, at] = (pj32[:, at] + term).astype(BF16)

    def project_cot(sub, side, first):
        at = pl.ds(pl.multiple_of(side * half, half), half)
        term = mm(xs[sub, 1, side], wo[sub, :, at], TAIL_CONTRACT)
        if first:
            ga32[...] = term
        else:
            ga[...] = (ga32[...] + term).astype(BF16)

    def attention(t, seq_mask):
        at = pl.ds(pl.multiple_of(t * half, half), half)
        at_out = pl.ds(pl.multiple_of(t * 2 * HD, 2 * HD), 2 * HD)
        for b in range(2):
            here = slice(b * block, (b + 1) * block)
            six = pj[here, at]
            two = ga[here, at_out]
            att_list, grad_list = [], []
            for i in range(2):
                q, k, v = [six[:, (3 * i + j) * HD : (3 * i + j + 1) * HD] for j in range(3)]
                attended, grads = attention_unit(q, k, v, two[:, i * HD : (i + 1) * HD], seq_mask)
                att_list.append(attended)
                grad_list += list(grads)
            att[here, at_out] = jnp.concatenate(att_list, -1).astype(BF16)
            gp[here, at] = jnp.concatenate(grad_list, -1).astype(BF16)

    def part_of(sub, side, f):
        at = pl.ds(pl.multiple_of(side * half + f * lanes, lanes), lanes)
        return mm(gp[...], wq[sub, at, :], TAIL_CONTRACT)

    def part_exchange(sub, f):
        return remote(
            psend.at[sub, f],
            precv.at[sub, f],
            part_sem.at[sub, f, 0],
            part_sem.at[sub, f, 1],
            pair,
        )

    def send_parts(sub):
        for f in range(cuts):
            psend[sub, f] = part_of(sub, o, f).astype(BF16)
            part_exchange(sub, f).start()

    def cut(f):
        return slice(f * lanes, (f + 1) * lanes)

    core = lax.rem(s, 2)
    xbit = lax.rem(s // 2, 2)
    z = s // 4
    zs = seq // 4
    chunk = 2 * half // seq

    def grads(sub, p):
        if isinstance(p, int) and p == tiles:
            a, right = 1, att[...]
        else:
            a, right = 0, gp[:, pl.ds(pl.multiple_of(p * half, half), half)]
        for side in range(2):
            term = mm(xt[sub, a, side], right).astype(BF16)
            gs[sub, p, side] = term.reshape(seq // 4, 2, chunk, half)

    def rs_first(sub, p):
        return remote(
            gs.at[sub, p, :, :, 1 - core],
            t1r.at[sub, p],
            rs12.at[sub, p, 0],
            rs12.at[sub, p, 1],
            at_seq(s + 1 - 2 * core),
        )

    def rs_second(sub, p):
        return remote(
            t1.at[sub, p, :, 1 - xbit],
            t2r.at[sub, p],
            rs12.at[sub, p, 2],
            rs12.at[sub, p, 3],
            at_seq(s + 2 - 4 * xbit),
        )

    def rs_third(sub, p, k):
        to = lax.rem(z + k, zs)
        return remote(
            t2.at[sub, p, to],
            t3r.at[sub, p, k - 1],
            rs3_s.at[sub, p, k - 1],
            rs3_r.at[sub, p, k - 1],
            at_seq(to * 4 + lax.rem(s, 4)),
        )

    def rs_after_first(sub, p):
        rs_first(sub, p).wait_recv()
        for side in range(2):
            for c in range(seq // 4):
                at = side * (seq // 4) + c
                total = gs[sub, p, side, c, core].astype(F32) + t1r[sub, p, side, c].astype(F32)
                t1[sub, p, at // 2, at % 2] = total.astype(BF16)
        rs_second(sub, p).start()

    def rs_after_second(sub, p):
        rs_second(sub, p).wait_recv()
        for c in range(zs):
            total = t1[sub, p, c, xbit].astype(F32) + t2r[sub, p, c].astype(F32)
            t2[sub, p, c] = total.astype(BF16)
        for k in range(1, zs):
            rs_third(sub, p, k).start()

    def rs_finish(sub, p, q_out, o_out):
        total = t2[sub, p, z].astype(F32)
        for k in range(1, zs):
            rs_third(sub, p, k).wait_recv()
            total = total + t3r[sub, p, k - 1].astype(F32)
        if p == tiles:
            o_out[...] = total
        else:
            q_out[:, p * half : (p + 1) * half] = total

    loads[0].wait()
    loads[1].wait()
    to_blocks(h)
    project(0, h, True)
    project_cot(0, h, True)
    turn(0, 0, h)
    turn(0, 1, h)

    @pl.loop(0, seq)
    def _(k):
        for a in range(2):
            forward(a, k).wait_recv()

    to_blocks(o)
    project(0, o, False)
    project_cot(0, o, False)
    row_ids = lax.broadcasted_iota(jnp.int32, (block, block), 0)
    col_ids = lax.broadcasted_iota(jnp.int32, (block, block), 1)
    lane = span // 2
    seq_mask = lax.rem(row_ids, lane) == lax.rem(col_ids, lane)

    @pl.loop(0, tiles)
    def _(t):
        attention(t, seq_mask)

    send_parts(0)
    for f in range(cuts):
        keep[:, cut(f)] = part_of(0, h, f)
    turn(0, 0, o)
    turn(0, 1, o)

    def give_back(f, k):
        peer = lax.rem(s + k, seq)
        return remote(
            rb.at[f, pl.ds(peer * rows, rows)],
            back.at[f, :, pl.ds(pl.multiple_of(s * span, span), span), :],
            back_s.at[f, k],
            back_r.at[f, k],
            at_seq(peer),
        )

    back_own = []
    for f in range(cuts):
        part_exchange(0, f).wait_recv()
        for b in range(2):
            here = slice(b * block, (b + 1) * block)
            total = keep[here, cut(f)] + precv[0, f, here, :].astype(F32)
            order[:, b * lane : (b + 1) * lane, :] = total.reshape(block // lane, lane, lanes)
        rb[f] = order[...].astype(BF16)

        @pl.loop(1, seq)
        def _(k):
            give_back(f, k).start()

        back_own.append(
            pltpu.make_async_copy(
                rb.at[f, pl.ds(s * rows, rows)],
                back.at[f, :, pl.ds(pl.multiple_of(s * span, span), span), :],
                lsem.at[3 + f],
            )
        )
        back_own[f].start()
        grads(0, f)

    def send_mid(f):
        return remote(
            mid.at[f], xs.at[1, 1, h, :, cut(f)], mid_sem.at[f, 0], mid_sem.at[f, 1], pair
        )

    for f in range(cuts):
        back_own[f].wait()

        @pl.loop(1, seq)
        def _(k):
            give_back(f, k).wait_recv()

        for r in range(rows):
            here = slice(r * bins, (r + 1) * bins)
            new = (cot_ref[r, :, cut(f)].astype(F32) + back[f, r].astype(F32)).astype(BF16)
            mid[f, here, :] = new
            xs[1, 1, h, here, cut(f)] = new
        send_mid(f).start()

    for p in range(cuts, pieces):
        grads(0, p)
    for p in range(pieces):
        rs_first(0, p).start()
    loads[2].wait()
    loads[3].wait()
    dop_own.wait()
    project(1, h, True)
    project_cot(1, h, True)
    for p in range(pieces):
        rs_after_first(0, p)
    dop_send.wait_recv()
    project(1, o, False)
    for side in range(2):
        turn(1, 0, side)
    turn(1, 1, h)
    for f in range(cuts):
        send_mid(f).wait_recv()
    project_cot(1, o, False)
    for p in range(pieces):
        rs_after_second(0, p)

    @pl.loop(0, tiles)
    def _(t):
        attention(t, None)
        grads(1, t)
        rs_first(1, t).start()

        @pl.when(t >= 1)
        def _():
            rs_after_first(1, t - 1)

        @pl.when(t >= 2)
        def _():
            rs_after_second(1, t - 2)

    send_parts(1)
    rs_after_first(1, tiles - 1)
    turn(1, 1, o)
    grads(1, tiles)
    rs_first(1, tiles).start()
    for f in range(cuts):
        keep[:, cut(f)] = part_of(1, h, f)
    for p in range(max(tiles - 2, 0), tiles - 1):
        rs_after_second(1, p)
    rs_after_first(1, tiles)
    for p in range(pieces):
        rs_finish(0, p, qr_ref, or_ref)
    for p in range(tiles - 1, pieces):
        rs_after_second(1, p)
    for f in range(cuts):
        part_exchange(1, f).wait_recv()
        added = (keep[:, cut(f)] + precv[1, f].astype(F32)).astype(BF16).astype(F32)
        ig_ref[:, cut(f)] = (mid[f].astype(F32) + added).astype(BF16)
    for p in range(pieces):
        rs_finish(1, p, qd_ref, od_ref)

    @pl.loop(1, seq)
    def _(k):
        for a in range(2):
            exchange(a, k).wait_send()
        for f in range(cuts):
            give_back(f, k).wait_send()

    @pl.loop(0, seq)
    def _(k):
        for a in range(2):
            forward(a, k).wait_send()

    dop_send.wait_send()
    for f in range(cuts):
        send_mid(f).wait_send()
    for sub in range(2):
        for f in range(cuts):
            part_exchange(sub, f).wait_send()
        for p in range(pieces):
            rs_first(sub, p).wait_send()
            rs_second(sub, p).wait_send()
            for k in range(1, zs):
                rs_third(sub, p, k).wait_send()


def emit_kernel(ig, qd, od, qr, out_r, ig_ref, qd_ref, od_ref, qr_ref, or_ref):
    ig_ref[...] = ig[...]
    qd_ref[...] = qd[...]
    od_ref[...] = od[...].T
    qr_ref[...] = qr[...]
    or_ref[...] = out_r[...].T


def shards_by_head(
    doppler_input, range_saved_input, layer_cot, qkv_doppler, out_doppler, qkv_range, out_range
):
    seq = lax.axis_size("seq")
    rows, bins, half = layer_cot.shape
    tokens = rows * bins
    cols = qkv_range.shape[1]
    chunk = 2 * half // seq
    lanes = 128
    cuts = half // lanes
    pieces = cols // half + 1
    span = bins // seq
    dma = pltpu.SemaphoreType.DMA
    vmem = pl.BlockSpec(memory_space=pltpu.VMEM)
    hbm = pl.BlockSpec(memory_space=pl.ANY)
    zs = seq // 4
    scratch = [
        pltpu.VMEM((2, 2 * half, cols), BF16),
        pltpu.VMEM((2, half, 2 * half), BF16),
        pltpu.VMEM((2, 2, rows * seq, span, half), BF16),
        pltpu.VMEM((2, 2, 2, tokens, half), BF16),
        pltpu.VMEM((2, 2, 2, half, tokens), BF16),
        pltpu.VMEM((tokens, cols), F32),
        pltpu.VMEM((tokens, half), F32),
        pltpu.VMEM((tokens, cols), BF16),
        pltpu.VMEM((tokens, half), BF16),
        pltpu.VMEM((tokens, cols), BF16),
        pltpu.VMEM((tokens, half), BF16),
        pltpu.VMEM((tokens, half), F32),
        pltpu.VMEM((2, cuts, tokens, lanes), BF16),
        pltpu.VMEM((2, cuts, tokens, lanes), BF16),
        pltpu.VMEM((rows * seq, span, lanes), F32),
        pltpu.VMEM((cuts, rows * seq, span, lanes), BF16),
        pltpu.VMEM((cuts, rows, bins, lanes), BF16),
        pltpu.VMEM((cuts, tokens, lanes), BF16),
        pltpu.VMEM((2, pieces, 2, seq // 4, 2, chunk, half), BF16),
        pltpu.VMEM((2, pieces, 2, seq // 4, chunk, half), BF16),
        pltpu.VMEM((2, pieces, zs, 2, chunk, half), BF16),
        pltpu.VMEM((2, pieces, zs, chunk, half), BF16),
        pltpu.VMEM((2, pieces, zs, chunk, half), BF16),
        pltpu.VMEM((2, pieces, zs - 1, chunk, half), BF16),
        dma((4,)),
        dma((3 + cuts,)),
        dma((2, seq)),
        dma((2, seq)),
        dma((2, seq)),
        dma((2, seq)),
        dma((2,)),
        dma((2, cuts, 2)),
        dma((cuts, seq)),
        dma((cuts, seq)),
        dma((cuts, 2)),
        dma((2, pieces, 4)),
        dma((2, pieces, zs - 1)),
        dma((2, pieces, zs - 1)),
    ]
    results = pl.pallas_call(
        functools.partial(layer_kernel, seq),
        out_shape=(
            jax.ShapeDtypeStruct((tokens, half), BF16),
            jax.ShapeDtypeStruct((chunk, cols), F32),
            jax.ShapeDtypeStruct((chunk, half), F32),
            jax.ShapeDtypeStruct((chunk, cols), F32),
            jax.ShapeDtypeStruct((chunk, half), F32),
        ),
        in_specs=[vmem] * 3 + [hbm] * 4,
        out_specs=(vmem,) * 5,
        scratch_shapes=scratch,
        compiler_params=pltpu.CompilerParams(
            collective_id=0, has_side_effects=True, vmem_limit_bytes=56 * 2**20
        ),
        name="axial_backward",
    )(
        doppler_input.reshape(tokens, half),
        range_saved_input,
        layer_cot,
        qkv_doppler,
        out_doppler,
        qkv_range,
        out_range,
    )
    ig, qd, od, qr, out_r = pl.pallas_call(
        emit_kernel,
        out_shape=(
            jax.ShapeDtypeStruct((tokens, half), BF16),
            jax.ShapeDtypeStruct((chunk, cols), F32),
            jax.ShapeDtypeStruct((half, chunk), F32),
            jax.ShapeDtypeStruct((chunk, cols), F32),
            jax.ShapeDtypeStruct((half, chunk), F32),
        ),
        in_specs=[vmem] * 5,
        out_specs=(vmem,) * 5,
        name="write_results",
    )(*results)
    return (ig.reshape(layer_cot.shape), qd, od, qr, out_r)


def by_head(mesh):
    return mesh.shape["head"] == 2 and mesh.shape["seq"] == 16


def solution(mesh):
    placed = (
        P("seq", None, "head"),
        P("seq", None, "head"),
        P("seq", None, "head"),
        P(None, "head"),
        P("head", None),
        P(None, "head"),
        P("head", None),
    )
    return jax.shard_map(
        shards_by_head if by_head(mesh) else shards,
        mesh=mesh,
        in_specs=placed,
        out_specs=(
            P("seq", None, "head"),
            P("seq", "head"),
            P("head", "seq"),
            P("seq", "head"),
            P("head", "seq"),
        ),
        check_vma=False,
    )
```

```python
import functools

import jax
import jax.numpy as jnp
from jax import lax
from jax.experimental import pallas as pl
from jax.experimental.pallas import tpu as pltpu
from jax.sharding import PartitionSpec as P

HD = 64


DOPPLER_SHAPES = ("asu,avu->asv", "ojs,ost->ojt", "aru,ary->auy")
RANGE_SHAPES = ("mpw,cpw->pmc", "fdv,vfo->dfo", "nhr,hnp->rnp")
LEAD_CONTRACT = (((0,), (0,)), ((), ()))
TAIL_CONTRACT = (((1,), (1,)), ((), ()))


def swapped(block, axis, stride):
    count = lax.axis_size(axis)
    route = []
    for low in range(count):
        high = low | 1 << stride
        if high != low and high < count:
            route += [(low, high), (high, low)]
    return lax.ppermute(block, axis, route)


def head_backward(query, keys, values, grad_attn, forms, scale):
    scores = jnp.einsum(forms[0], query, keys, preferred_element_type=jnp.float32) * scale
    scores = scores - jnp.max(scores, axis=-1, keepdims=True)
    expo = jnp.exp(scores)
    probs = expo / jnp.sum(expo, axis=-1, keepdims=True)
    probs_low = probs.astype(jnp.bfloat16)
    attended = jnp.einsum(forms[1], probs_low, values, preferred_element_type=jnp.float32).astype(
        jnp.bfloat16
    )
    grad_values = jnp.einsum(
        forms[2], probs_low, grad_attn, preferred_element_type=jnp.float32
    ).astype(jnp.bfloat16)
    grad_probs = jnp.einsum(forms[0], grad_attn, values, preferred_element_type=jnp.float32)
    grad_scores = (
        probs * (grad_probs - jnp.sum(probs * grad_probs, axis=-1, keepdims=True)) * scale
    ).astype(jnp.bfloat16)
    grad_query = jnp.einsum(forms[1], grad_scores, keys, preferred_element_type=jnp.float32).astype(
        jnp.bfloat16
    )
    grad_keys = jnp.einsum(forms[2], grad_scores, query, preferred_element_type=jnp.float32).astype(
        jnp.bfloat16
    )
    return (attended, grad_query, grad_keys, grad_values)


def sublayer_local(inputs, cotangent, weight_qkv, weight_out, forms):
    width = inputs.shape[-1]
    leading = inputs.shape[:-1]
    flat_in = inputs.reshape(-1, width)
    flat_cot = cotangent.reshape(-1, width)
    heads_here = weight_out.shape[0] // HD
    projection = jnp.dot(flat_in, weight_qkv, preferred_element_type=jnp.float32).astype(
        jnp.bfloat16
    )
    projection = projection.reshape(leading + (heads_here, 3, HD))
    grad_attn = lax.dot_general(
        flat_cot, weight_out, TAIL_CONTRACT, preferred_element_type=jnp.float32
    )
    grad_attn = grad_attn.astype(jnp.bfloat16).reshape(leading + (heads_here, HD))
    scale = HD ** (-0.5)
    attended_list = []
    grad_list = []
    for head_index in range(heads_here):
        attended, grad_query, grad_keys, grad_values = head_backward(
            projection[..., head_index, 0, :],
            projection[..., head_index, 1, :],
            projection[..., head_index, 2, :],
            grad_attn[..., head_index, :],
            forms,
            scale,
        )
        attended_list.append(attended)
        grad_list.append(jnp.stack([grad_query, grad_keys, grad_values], axis=-2))
    attended = jnp.stack(attended_list, axis=-2).reshape(-1, heads_here * HD)
    grad_proj = jnp.stack(grad_list, axis=-3).reshape(-1, 3 * heads_here * HD)
    out_term = lax.dot_general(
        attended, flat_cot, LEAD_CONTRACT, preferred_element_type=jnp.float32
    )
    qkv_term = lax.dot_general(
        flat_in, grad_proj, LEAD_CONTRACT, preferred_element_type=jnp.float32
    )
    group_part = lax.dot_general(
        grad_proj, weight_qkv, TAIL_CONTRACT, preferred_element_type=jnp.float32
    )
    return (group_part.astype(jnp.bfloat16).reshape(inputs.shape), qkv_term, out_term)


def pair_weights(weight_qkv, weight_out, lower_half):
    other_qkv = swapped(weight_qkv, "head", 0)
    other_out = swapped(weight_out, "head", 0)
    full_qkv = jnp.where(
        lower_half,
        jnp.concatenate([weight_qkv, other_qkv], 1),
        jnp.concatenate([other_qkv, weight_qkv], 1),
    )
    full_out = jnp.where(
        lower_half,
        jnp.concatenate([weight_out, other_out], 0),
        jnp.concatenate([other_out, weight_out], 0),
    )
    return (full_qkv, full_out)


def reduction_terms(qkv_term, out_term, lower_half):
    half_width = qkv_term.shape[1] // 2
    half_rows = out_term.shape[0] // 2
    qkv_low, qkv_high = (qkv_term[:, :half_width], qkv_term[:, half_width:])
    out_low, out_high = (out_term[:half_rows], out_term[half_rows:])
    qkv_keep = jnp.where(lower_half, qkv_low, qkv_high)
    qkv_send = jnp.where(lower_half, qkv_high, qkv_low)
    out_keep = jnp.where(lower_half, out_low, out_high)
    out_send = jnp.where(lower_half, out_high, out_low)
    qkv_term = qkv_keep + swapped(qkv_send.astype(jnp.bfloat16), "head", 0).astype(qkv_send.dtype)
    out_term = out_keep + swapped(out_send.astype(jnp.bfloat16), "head", 0).astype(out_send.dtype)
    return (
        lax.psum_scatter(qkv_term, "seq", scatter_dimension=0, tiled=True),
        lax.psum_scatter(out_term, "seq", scatter_dimension=1, tiled=True),
    )


def shards(
    doppler_input, range_saved_input, layer_cot, qkv_doppler, out_doppler, qkv_range, out_range
):
    head_count = lax.axis_size("head")
    group_count = head_count // 2
    split_count = head_count // group_count
    position = lax.axis_index("head") % split_count
    lower_half = position == 0
    range_qkv, range_out = pair_weights(qkv_range, out_range, lower_half)
    doppler_qkv, doppler_out = pair_weights(qkv_doppler, out_doppler, lower_half)
    full_mid, full_cot = (
        lax.all_gather(range_saved_input, "head", axis=2, tiled=True),
        lax.all_gather(layer_cot, "head", axis=2, tiled=True),
    )
    column_middle, column_cot = (
        lax.all_to_all(full_mid, "seq", split_axis=1, concat_axis=0, tiled=True),
        lax.all_to_all(full_cot, "seq", split_axis=1, concat_axis=0, tiled=True),
    )
    part_width = column_middle.shape[1] // split_count
    column_start = position * part_width
    local_mid = lax.dynamic_slice_in_dim(column_middle, column_start, part_width, 1)
    local_cot = lax.dynamic_slice_in_dim(column_cot, column_start, part_width, 1)
    range_part, qkv_term, out_term = sublayer_local(
        local_mid, local_cot, range_qkv, range_out, RANGE_SHAPES
    )
    qkv_range_grad, out_range_grad = reduction_terms(qkv_term, out_term, lower_half)
    column_moved = lax.all_to_all(range_part, "head", split_axis=2, concat_axis=1, tiled=True)
    column_moved = column_moved.reshape(
        column_moved.shape[0], group_count, -1, column_moved.shape[2]
    )
    range_back = jnp.sum(column_moved, axis=1, dtype=jnp.float32).astype(jnp.bfloat16)
    row_backward_result = lax.all_to_all(range_back, "seq", split_axis=0, concat_axis=1, tiled=True)
    cotangent_mid = (
        layer_cot.astype(jnp.float32) + row_backward_result.astype(jnp.float32)
    ).astype(jnp.bfloat16)
    full_in, full_cot_mid = (
        lax.all_gather(doppler_input, "head", axis=2, tiled=True),
        lax.all_gather(cotangent_mid, "head", axis=2, tiled=True),
    )
    part_rows = full_in.shape[0] // split_count
    row_start = position * part_rows
    local_in = lax.dynamic_slice_in_dim(full_in, row_start, part_rows, 0)
    local_cot_mid = lax.dynamic_slice_in_dim(full_cot_mid, row_start, part_rows, 0)
    doppler_part, qkv_term, out_term = sublayer_local(
        local_in, local_cot_mid, doppler_qkv, doppler_out, DOPPLER_SHAPES
    )
    qkv_doppler_grad, out_doppler_grad = reduction_terms(qkv_term, out_term, lower_half)
    row_moved = lax.all_to_all(doppler_part, "head", split_axis=2, concat_axis=0, tiled=True)
    row_moved = row_moved.reshape(group_count, -1, row_moved.shape[1], row_moved.shape[2])
    doppler_back = jnp.sum(row_moved, axis=0, dtype=jnp.float32)
    input_grad = (cotangent_mid.astype(jnp.float32) + doppler_back).astype(jnp.bfloat16)
    return (input_grad, qkv_doppler_grad, out_doppler_grad, qkv_range_grad, out_range_grad)


MESH = pl.DeviceIdType.MESH
F32 = jnp.float32
BF16 = jnp.bfloat16
PLAIN = (((1,), (0,)), ((), ()))
HIDDEN = -1e30


def mm(a, b, form=PLAIN):
    return lax.dot_general(a, b, form, preferred_element_type=F32)


def attention_unit(query, keys, values, grad_attn, seq_mask):
    scale = HD ** (-0.5)
    scores = mm(query, keys, TAIL_CONTRACT) * scale
    if seq_mask is not None:
        scores = jnp.where(seq_mask, scores, HIDDEN)
    expo = jnp.exp(scores - jnp.max(scores, axis=-1, keepdims=True))
    probs = expo * (1.0 / jnp.sum(expo, axis=-1, keepdims=True))
    probs_low = probs.astype(BF16)
    attended = mm(probs_low, values)
    grad_values = mm(probs_low, grad_attn, LEAD_CONTRACT)
    grad_probs = mm(grad_attn, values, TAIL_CONTRACT)
    dots = jnp.sum(probs * grad_probs, axis=-1, keepdims=True)
    grad_scores = (probs * (grad_probs - dots) * scale).astype(BF16)
    grad_query = mm(grad_scores, keys)
    grad_keys = mm(grad_scores, query, LEAD_CONTRACT)
    return attended, (grad_query, grad_keys, grad_values)


def layer_kernel(
    seq,
    dop_ref,
    rng_ref,
    cot_ref,
    wqd_hbm,
    wod_hbm,
    wqr_hbm,
    wor_hbm,
    ig_ref,
    qd_ref,
    od_ref,
    qr_ref,
    or_ref,
    wq,
    wo,
    xr,
    xs,
    xt,
    pj32,
    ga32,
    pj,
    ga,
    gp,
    att,
    keep,
    psend,
    precv,
    order,
    rb,
    back,
    mid,
    gs,
    t1r,
    t1,
    t2r,
    t2,
    t3r,
    wsem,
    lsem,
    a2a_s,
    a2a_r,
    fwd_s,
    fwd_r,
    dx_sem,
    part_sem,
    back_s,
    back_r,
    mid_sem,
    rs12,
    rs3_s,
    rs3_r,
):
    s = lax.axis_index("seq")
    h = lax.axis_index("head")
    o = 1 - h
    rows, bins, half = rng_ref.shape
    span = bins // seq
    tokens = rows * bins
    block = tokens // 2
    pair = {"seq": s, "head": o}
    cols = wqr_hbm.shape[1]
    tiles = cols // half
    lanes = 128
    cuts = half // lanes
    pieces = tiles + 1

    core = lax.rem(s, 2)
    xbit = lax.rem(s // 2, 2)
    z = s // 4
    zs = seq // 4
    low = lax.rem(s, 4)

    def peer_of(k):
        return lax.rem(z + k // 4, zs) * 4 + lax.rem(low + lax.rem(k, 4), 4)

    def at_seq(q):
        return {"seq": q, "head": h}

    def remote(src, dst, send, recv, where):
        return pltpu.make_async_remote_copy(
            src_ref=src,
            dst_ref=dst,
            send_sem=send,
            recv_sem=recv,
            device_id=(where["seq"], where["head"]),
            device_id_type=MESH,
        )

    loads = [
        pltpu.make_async_copy(wqr_hbm, wq.at[0], wsem.at[0]),
        pltpu.make_async_copy(wor_hbm, wo.at[0], wsem.at[1]),
        pltpu.make_async_copy(wqd_hbm, wq.at[1], wsem.at[2]),
        pltpu.make_async_copy(wod_hbm, wo.at[1], wsem.at[3]),
    ]
    for load in loads:
        load.start()

    barrier = pltpu.get_barrier_semaphore()

    @pl.loop(1, seq)
    def _(k):
        pl.semaphore_signal(
            barrier, inc=1, device_id=(peer_of(k), h), device_id_type=MESH
        )

    pl.semaphore_signal(barrier, inc=1, device_id=(s, o), device_id_type=MESH)
    pl.semaphore_wait(barrier, seq)

    sources = (rng_ref, cot_ref)

    def exchange(a, k):
        peer = peer_of(k)
        return remote(
            sources[a].at[:, pl.ds(pl.multiple_of(peer * span, span), span), :],
            xr.at[a, h, pl.ds(s * rows, rows)],
            a2a_s.at[a, k],
            a2a_r.at[a, k],
            at_seq(peer),
        )

    def forward(a, k):
        origin = lax.rem(z - k // 4 + zs, zs) * 4 + lax.rem(low - lax.rem(k, 4) + 4, 4)
        place = xr.at[a, h, pl.ds(origin * rows, rows)]
        return remote(place, place, fwd_s.at[a, k], fwd_r.at[a, k], pair)

    @pl.loop(1, seq)
    def _(k):
        for a in range(2):
            exchange(a, k).start()

    for a in range(2):
        own = pltpu.make_async_copy(
            sources[a].at[:, pl.ds(pl.multiple_of(s * span, span), span), :],
            xr.at[a, h, pl.ds(s * rows, rows)],
            lsem.at[a],
        )
        own.start()
        own.wait()
        forward(a, 0).start()

    dop_own = pltpu.make_async_copy(dop_ref, xs.at[1, 0, h], lsem.at[2])
    dop_own.start()

    def forward_arrived(first, last):
        @pl.loop(first, last)
        def _(k):
            for a in range(2):
                exchange(a, k).wait_recv()
                forward(a, k).start()

    def to_blocks(side):
        for a in range(2):
            moved = xr[a, side].astype(F32)
            for b in range(2):
                piece = moved[:, b * (span // 2) : (b + 1) * (span // 2), :]
                xs[0, a, side, b * block : (b + 1) * block, :] = piece.reshape(
                    block, half
                ).astype(BF16)

    def turn(sub, a, side):
        xt[sub, a, side] = xs[sub, a, side].T

    def project(sub, side, first):
        @pl.loop(0, tiles)
        def _(t):
            at = pl.ds(pl.multiple_of(t * half, half), half)
            term = mm(xs[sub, 0, side], wq[sub, pl.ds(pl.multiple_of(side * half, half), half), at])
            if first:
                pj32[sub, :, at] = term
            else:
                pj[:, at] = (pj32[sub, :, at] + term).astype(BF16)

    def project_cot(sub, side, first):
        at = pl.ds(pl.multiple_of(side * half, half), half)
        term = mm(xs[sub, 1, side], wo[sub, :, at], TAIL_CONTRACT)
        if first:
            ga32[...] = term
        else:
            ga[...] = (ga32[...] + term).astype(BF16)

    def attention(t, seq_mask):
        at = pl.ds(pl.multiple_of(t * half, half), half)
        at_out = pl.ds(pl.multiple_of(t * 2 * HD, 2 * HD), 2 * HD)
        for b in range(2):
            here = slice(b * block, (b + 1) * block)
            six = pj[here, at]
            two = ga[here, at_out]
            att_list, grad_list = [], []
            for i in range(2):
                q, k, v = [six[:, (3 * i + j) * HD : (3 * i + j + 1) * HD] for j in range(3)]
                attended, grads = attention_unit(q, k, v, two[:, i * HD : (i + 1) * HD], seq_mask)
                att_list.append(attended)
                grad_list += list(grads)
            att[here, at_out] = jnp.concatenate(att_list, -1).astype(BF16)
            gp[here, at] = jnp.concatenate(grad_list, -1).astype(BF16)

    def part_of(sub, side, f):
        at = pl.ds(pl.multiple_of(side * half + f * lanes, lanes), lanes)
        return mm(gp[...], wq[sub, at, :], TAIL_CONTRACT)

    def part_whole(sub, side):
        at = pl.ds(pl.multiple_of(side * half, half), half)
        return mm(gp[...], wq[sub, at, :], TAIL_CONTRACT)

    def part_exchange(sub, f):
        return remote(
            psend.at[sub, f],
            precv.at[sub, f],
            part_sem.at[sub, f, 0],
            part_sem.at[sub, f, 1],
            pair,
        )

    def send_parts(sub):
        for f in range(cuts):
            psend[sub, f] = part_of(sub, o, f).astype(BF16)
            part_exchange(sub, f).start()

    def cut(f):
        return slice(f * lanes, (f + 1) * lanes)

    chunk = 2 * half // seq

    def grads(sub, p):
        if isinstance(p, int) and p == tiles:
            a, right = 1, att[...]
        else:
            a, right = 0, gp[:, pl.ds(pl.multiple_of(p * half, half), half)]
        for side in range(2):
            term = mm(xt[sub, a, side], right).astype(BF16)
            gs[sub, p, side] = term.reshape(seq // 4, 2, chunk, half)

    def rs_first(sub, p):
        return remote(
            gs.at[sub, p, :, :, 1 - core],
            t1r.at[sub, p],
            rs12.at[sub, p, 0],
            rs12.at[sub, p, 1],
            at_seq(s + 1 - 2 * core),
        )

    def rs_second(sub, p):
        return remote(
            t1.at[sub, p, :, 1 - xbit],
            t2r.at[sub, p],
            rs12.at[sub, p, 2],
            rs12.at[sub, p, 3],
            at_seq(s + 2 - 4 * xbit),
        )

    def rs_third(sub, p, k):
        to = lax.rem(z + k, zs)
        return remote(
            t2.at[sub, p, to],
            t3r.at[sub, p, k - 1],
            rs3_s.at[sub, p, k - 1],
            rs3_r.at[sub, p, k - 1],
            at_seq(to * 4 + lax.rem(s, 4)),
        )

    def rs_after_first(sub, p):
        rs_first(sub, p).wait_recv()
        for side in range(2):
            for c in range(seq // 4):
                at = side * (seq // 4) + c
                total = gs[sub, p, side, c, core].astype(F32) + t1r[sub, p, side, c].astype(F32)
                t1[sub, p, at // 2, at % 2] = total.astype(BF16)
        rs_second(sub, p).start()

    def rs_after_second(sub, p):
        rs_second(sub, p).wait_recv()
        for c in range(zs):
            total = t1[sub, p, c, xbit].astype(F32) + t2r[sub, p, c].astype(F32)
            t2[sub, p, c] = total.astype(BF16)
        for k in range(1, zs):
            rs_third(sub, p, k).start()

    def rs_finish(sub, p, q_out, o_out):
        total = t2[sub, p, z].astype(F32)
        for k in range(1, zs):
            rs_third(sub, p, k).wait_recv()
            total = total + t3r[sub, p, k - 1].astype(F32)
        if p == tiles:
            o_out[...] = total
        else:
            q_out[:, p * half : (p + 1) * half] = total

    forward_arrived(1, 4)
    for load in loads:
        load.wait()
    dop_own.wait()
    project(1, h, True)
    turn(1, 0, h)
    forward_arrived(4, seq)
    dop_send = remote(dop_ref, xs.at[1, 0, h], dx_sem.at[0], dx_sem.at[1], pair)
    dop_send.start()
    to_blocks(h)
    project(0, h, True)
    project_cot(0, h, True)
    turn(0, 0, h)
    turn(0, 1, h)

    @pl.loop(0, seq)
    def _(k):
        for a in range(2):
            forward(a, k).wait_recv()

    to_blocks(o)
    project(0, o, False)
    project_cot(0, o, False)
    row_ids = lax.broadcasted_iota(jnp.int32, (block, block), 0)
    col_ids = lax.broadcasted_iota(jnp.int32, (block, block), 1)
    lane = span // 2
    seq_mask = lax.rem(row_ids, lane) == lax.rem(col_ids, lane)

    @pl.loop(0, tiles)
    def _(t):
        attention(t, seq_mask)

    send_parts(0)
    keep[...] = part_whole(0, h)
    turn(0, 0, o)
    turn(0, 1, o)

    def give_back(f, k):
        peer = peer_of(k)
        return remote(
            rb.at[f, pl.ds(peer * rows, rows)],
            back.at[f, :, pl.ds(pl.multiple_of(s * span, span), span), :],
            back_s.at[f, k],
            back_r.at[f, k],
            at_seq(peer),
        )

    back_own = []
    for f in range(cuts):
        part_exchange(0, f).wait_recv()
        for b in range(2):
            here = slice(b * block, (b + 1) * block)
            total = keep[here, cut(f)] + precv[0, f, here, :].astype(F32)
            order[:, b * lane : (b + 1) * lane, :] = total.reshape(block // lane, lane, lanes)
        rb[f] = order[...].astype(BF16)

        @pl.loop(1, seq)
        def _(k):
            give_back(f, k).start()

        back_own.append(
            pltpu.make_async_copy(
                rb.at[f, pl.ds(s * rows, rows)],
                back.at[f, :, pl.ds(pl.multiple_of(s * span, span), span), :],
                lsem.at[3 + f],
            )
        )
        back_own[f].start()
        grads(0, f)
        rs_first(0, f).start()

    grads(0, tiles)
    rs_first(0, tiles).start()

    def send_mid(f):
        return remote(
            mid.at[f], xs.at[1, 1, h, :, cut(f)], mid_sem.at[f, 0], mid_sem.at[f, 1], pair
        )

    for f in range(cuts):
        back_own[f].wait()

        @pl.loop(1, seq)
        def _(k):
            give_back(f, k).wait_recv()

        for r in range(rows):
            here = slice(r * bins, (r + 1) * bins)
            new = (cot_ref[r, :, cut(f)].astype(F32) + back[f, r].astype(F32)).astype(BF16)
            mid[f, here, :] = new
            xs[1, 1, h, here, cut(f)] = new
        send_mid(f).start()
        rs_after_first(0, f)

    project_cot(1, h, True)
    rs_after_first(0, tiles)
    dop_send.wait_recv()
    project(1, o, False)
    for p in range(cuts):
        rs_after_second(0, p)
    turn(1, 0, o)
    turn(1, 1, h)
    for f in range(cuts):
        send_mid(f).wait_recv()
    project_cot(1, o, False)
    turn(1, 1, o)
    rs_after_second(0, tiles)

    @pl.loop(0, tiles)
    def _(t):
        attention(t, None)
        grads(1, t)
        rs_first(1, t).start()

        @pl.when(t >= 1)
        def _():
            rs_after_first(1, t - 1)

        @pl.when(t >= 2)
        def _():
            rs_after_second(1, t - 2)

    grads(1, tiles)
    rs_first(1, tiles).start()
    rs_after_first(1, tiles - 1)
    send_parts(1)
    rs_after_first(1, tiles)
    for p in range(max(tiles - 2, 0), tiles - 1):
        rs_after_second(1, p)
    keep[...] = part_whole(1, h)
    rs_after_second(1, tiles - 1)
    for p in range(pieces):
        rs_finish(0, p, qr_ref, or_ref)
    rs_after_second(1, tiles)
    for f in range(cuts):
        part_exchange(1, f).wait_recv()
        added = (keep[:, cut(f)] + precv[1, f].astype(F32)).astype(BF16).astype(F32)
        ig_ref[:, cut(f)] = (mid[f].astype(F32) + added).astype(BF16)
    for p in range(pieces):
        rs_finish(1, p, qd_ref, od_ref)

    @pl.loop(1, seq)
    def _(k):
        for a in range(2):
            exchange(a, k).wait_send()
        for f in range(cuts):
            give_back(f, k).wait_send()

    @pl.loop(0, seq)
    def _(k):
        for a in range(2):
            forward(a, k).wait_send()

    dop_send.wait_send()
    for f in range(cuts):
        send_mid(f).wait_send()
    for sub in range(2):
        for f in range(cuts):
            part_exchange(sub, f).wait_send()
        for p in range(pieces):
            rs_first(sub, p).wait_send()
            rs_second(sub, p).wait_send()
            for k in range(1, zs):
                rs_third(sub, p, k).wait_send()


def emit_kernel(ig, qd, od, qr, out_r, ig_ref, qd_ref, od_ref, qr_ref, or_ref):
    ig_ref[...] = ig[...]
    qd_ref[...] = qd[...]
    od_ref[...] = od[...]
    qr_ref[...] = qr[...]
    or_ref[...] = out_r[...]


def shards_by_head(
    doppler_input, range_saved_input, layer_cot, qkv_doppler, out_doppler, qkv_range, out_range
):
    seq = lax.axis_size("seq")
    rows, bins, half = layer_cot.shape
    tokens = rows * bins
    cols = qkv_range.shape[1]
    chunk = 2 * half // seq
    lanes = 128
    cuts = half // lanes
    pieces = cols // half + 1
    span = bins // seq
    dma = pltpu.SemaphoreType.DMA
    vmem = pl.BlockSpec(memory_space=pltpu.VMEM)
    hbm = pl.BlockSpec(memory_space=pl.ANY)
    zs = seq // 4
    scratch = [
        pltpu.VMEM((2, 2 * half, cols), BF16),
        pltpu.VMEM((2, half, 2 * half), BF16),
        pltpu.VMEM((2, 2, rows * seq, span, half), BF16),
        pltpu.VMEM((2, 2, 2, tokens, half), BF16),
        pltpu.VMEM((2, 2, 2, half, tokens), BF16),
        pltpu.VMEM((2, tokens, cols), F32),
        pltpu.VMEM((tokens, half), F32),
        pltpu.VMEM((tokens, cols), BF16),
        pltpu.VMEM((tokens, half), BF16),
        pltpu.VMEM((tokens, cols), BF16),
        pltpu.VMEM((tokens, half), BF16),
        pltpu.VMEM((tokens, half), F32),
        pltpu.VMEM((2, cuts, tokens, lanes), BF16),
        pltpu.VMEM((2, cuts, tokens, lanes), BF16),
        pltpu.VMEM((rows * seq, span, lanes), F32),
        pltpu.VMEM((cuts, rows * seq, span, lanes), BF16),
        pltpu.VMEM((cuts, rows, bins, lanes), BF16),
        pltpu.VMEM((cuts, tokens, lanes), BF16),
        pltpu.VMEM((2, pieces, 2, seq // 4, 2, chunk, half), BF16),
        pltpu.VMEM((2, pieces, 2, seq // 4, chunk, half), BF16),
        pltpu.VMEM((2, pieces, zs, 2, chunk, half), BF16),
        pltpu.VMEM((2, pieces, zs, chunk, half), BF16),
        pltpu.VMEM((2, pieces, zs, chunk, half), BF16),
        pltpu.VMEM((2, pieces, zs - 1, chunk, half), BF16),
        dma((4,)),
        dma((3 + cuts,)),
        dma((2, seq)),
        dma((2, seq)),
        dma((2, seq)),
        dma((2, seq)),
        dma((2,)),
        dma((2, cuts, 2)),
        dma((cuts, seq)),
        dma((cuts, seq)),
        dma((cuts, 2)),
        dma((2, pieces, 4)),
        dma((2, pieces, zs - 1)),
        dma((2, pieces, zs - 1)),
    ]
    results = pl.pallas_call(
        functools.partial(layer_kernel, seq),
        out_shape=(
            jax.ShapeDtypeStruct((tokens, half), BF16),
            jax.ShapeDtypeStruct((chunk, cols), F32),
            jax.ShapeDtypeStruct((chunk, half), F32),
            jax.ShapeDtypeStruct((chunk, cols), F32),
            jax.ShapeDtypeStruct((chunk, half), F32),
        ),
        in_specs=[vmem] * 3 + [hbm] * 4,
        out_specs=(vmem,) * 5,
        scratch_shapes=scratch,
        compiler_params=pltpu.CompilerParams(
            collective_id=0, has_side_effects=True, vmem_limit_bytes=56 * 2**20
        ),
        name="axial_backward",
    )(
        doppler_input.reshape(tokens, half),
        range_saved_input,
        layer_cot,
        qkv_doppler,
        out_doppler,
        qkv_range,
        out_range,
    )
    ig, qd, od, qr, out_r = pl.pallas_call(
        emit_kernel,
        out_shape=(
            jax.ShapeDtypeStruct((tokens, half), BF16),
            jax.ShapeDtypeStruct((chunk, cols), F32),
            jax.ShapeDtypeStruct((chunk, half), F32),
            jax.ShapeDtypeStruct((chunk, cols), F32),
            jax.ShapeDtypeStruct((chunk, half), F32),
        ),
        in_specs=[vmem] * 5,
        out_specs=(vmem,) * 5,
        name="write_results",
    )(*results)
    return (ig.reshape(layer_cot.shape), qd, od.T, qr, out_r.T)


def by_head(mesh):
    return mesh.shape["head"] == 2 and mesh.shape["seq"] == 16


def solution(mesh):
    placed = (
        P("seq", None, "head"),
        P("seq", None, "head"),
        P("seq", None, "head"),
        P(None, "head"),
        P("head", None),
        P(None, "head"),
        P("head", None),
    )
    return jax.shard_map(
        shards_by_head if by_head(mesh) else shards,
        mesh=mesh,
        in_specs=placed,
        out_specs=(
            P("seq", None, "head"),
            P("seq", "head"),
            P("head", "seq"),
            P("seq", "head"),
            P("head", "seq"),
        ),
        check_vma=False,
    )
```
